32 devices in a mesh: group: 2 (over y), outer: 2 (over core), inner: 8 (over z, x).
Axes of the slice: x: 2, y: 2, z: 4, core: 2. Of those that a mesh axis runs over, the one named last changes fastest.
Arguments:
- queries: bfloat16 [16384, 384], P(('group', 'outer', 'inner')), parts along dimension 0, may hold values from -6 to 6
- key_rows: bfloat16 [16384, 384], P(('group', 'outer', 'inner')), parts along dimension 0, may hold values from -6 to 6
- value_rows: bfloat16 [16384, 384], P(('group', 'outer', 'inner')), parts along dimension 0, may hold values from -6 to 6
- grad_out: bfloat16 [16384, 384], P(('group', 'outer', 'inner')), parts along dimension 0, may hold values from -96 to 96
Outputs:
- attended: bfloat16 [16384, 384], P(('group', 'outer', 'inner')), parts along dimension 0
- grad_query: bfloat16 [16384, 384], P(('group', 'outer', 'inner')), parts along dimension 0
- grad_key: bfloat16 [16384, 384], P(('group', 'outer', 'inner')), parts along dimension 0
- grad_value: bfloat16 [16384, 384], P(('group', 'outer', 'inner')), parts along dimension 0
The draws below stay inside these ranges and needn't reach their ends.
There are 2 independent parts, one for each index of `group`. The reference program is written for one: setup_inputs(seed, part) draws one part's arguments, and reference() takes and returns one part's arrays. A program takes and returns all parts, laid end to end along the dimension named above; each array names one. Nothing has to cross between parts.
All inputs are finite; a program needn't handle non-finite values.
Results may differ from the reference program's by a relative error of at most 0.0071.
Values may be sent and summed in bfloat16 or wider, within the bound.
A program may use at most 64 MiB of HBM per device.

```python
import jax
import jax.numpy as jnp
from jax import lax

H = 6
E = 64
W1 = 512
R1 = 4
W2 = 8192
R2 = 64
TOKENS = 8192
R3 = 16


def draw_queries(key, part):
    key = jax.random.fold_in(key, 11)
    matrix = jnp.clip(jax.random.normal(key, (TOKENS, H * E)), -6.0, 6.0)
    return matrix.astype(jnp.bfloat16)


def draw_key_rows(key, part):
    key = jax.random.fold_in(key, 23)
    matrix = jnp.clip(jax.random.normal(key, (TOKENS, H * E)), -6.0, 6.0)
    return matrix.astype(jnp.bfloat16)


def levels(own_key, dims, cuts, smallest, top_value):
    loudness = 1.0
    for dim, parts in cuts:
        draws = jax.random.uniform(jax.random.fold_in(jax.random.fold_in(own_key, 6), dim), (parts,), jnp.float32, smallest / len(cuts), top_value / len(cuts))
        loudness = loudness * jnp.repeat(jnp.exp(draws), dims[dim] // parts).reshape((-1,) + (1,) * (len(dims) - 1 - dim))
    return loudness


def gaussian(stream_key, extent, scale, reach, cuts=(), kind=jnp.bfloat16):
    array = scale * jax.random.normal(stream_key, extent, jnp.float32)
    if cuts:
        array = array * levels(stream_key, extent, cuts, -0.22, 0.18)
    return jnp.clip(array, -reach, reach).astype(kind)


def setup_inputs(seed: int = 0, part: int = 0) -> dict:
    keys = jax.random.split(jax.random.key(seed), 5)
    part_splits = jax.random.split(jax.random.fold_in(keys[4], part), 5)
    return {
        "queries": draw_queries(jax.random.fold_in(jax.random.fold_in(keys[4], part), 71), part),
        "key_rows": draw_key_rows(jax.random.fold_in(jax.random.fold_in(keys[4], part), 71), part),
        "value_rows": gaussian(part_splits[2], (TOKENS, H * E), 1.0, 6.0, ((0, 16),)),
        "grad_out": gaussian(part_splits[3], (TOKENS, H * E), 16.0, 96.0, ((0, 16),)),
    }


HIGHEST = lax.Precision.HIGHEST
NEGATIVE = -1e30


def product(form, left, right):
    return jnp.einsum(form, lax.optimization_barrier(left).astype(jnp.float32),
                      lax.optimization_barrier(right).astype(jnp.float32), precision=HIGHEST)


def pick(matrix, stride):
    length = matrix.shape[0]
    count = matrix.shape[1]
    folded = matrix.reshape((length // stride, stride) + matrix.shape[1:])
    return jnp.stack([folded[:, head % stride, head] for head in range(count)], axis=1)


def spread(matrix, stride, filler):
    count = matrix.shape[1]
    extra = (1,) * (matrix.ndim - 2)
    selector = (jnp.arange(stride)[:, None] == jnp.arange(count)[None, :] % stride).reshape((1, stride, count) + extra)
    placed = jnp.where(selector, matrix[:, None], filler)
    return placed.reshape((matrix.shape[0] * stride,) + matrix.shape[1:])


def part_stats(query_sel, key_sel, value_sel):
    scale = query_sel.shape[-1] ** -0.5
    scores = product("qhe,khe->hqk", query_sel, key_sel) * scale
    peak = jnp.max(scores, axis=-1)
    weights = jnp.exp(scores - peak[..., None])
    mass = jnp.sum(weights, axis=-1)
    summed = product("hqk,khe->qhe", weights.astype(jnp.bfloat16), value_sel)
    return peak.T, mass.T, summed


def part_grads(query_sel, key_sel, value_sel, grad_sel, log_sel, dot_sel):
    scale = query_sel.shape[-1] ** -0.5
    scores = product("qhe,khe->hqk", query_sel, key_sel) * scale
    weights = jnp.exp(scores - log_sel.T[:, :, None])
    grad_v = product("hqk,qhe->khe", weights.astype(jnp.bfloat16), grad_sel)
    grad_w = product("qhe,khe->hqk", grad_sel, value_sel)
    grad_s = (weights * (grad_w - dot_sel.T[:, :, None]) * scale).astype(jnp.bfloat16)
    grad_q = product("hqk,khe->qhe", grad_s, key_sel)
    grad_k = product("hqk,qhe->khe", grad_s, query_sel)
    return grad_q, grad_k, grad_v


def run_stats(items):
    return part_stats(*items)


def run_grads(items):
    return part_grads(*items)


def reference(queries, key_rows, value_rows, grad_out):
    total = queries.shape[0]
    query_heads = queries.reshape(total, H, E)
    key_heads = key_rows.reshape(total, H, E)
    value_heads = value_rows.reshape(total, H, E)
    grad_heads = grad_out.reshape(total, H, E)
    configs = ((R1, W1), (R2, W2), (R3, total))

    def segmented(matrix, stride, segment):
        return pick(matrix, stride).reshape((total // segment, segment // stride) + matrix.shape[1:])

    def placed(matrix, stride, filler):
        return spread(matrix.reshape((total // stride,) + matrix.shape[2:]), stride, filler)

    peak_list, mass_list, summed_list = [], [], []
    for stride, segment in configs:
        peak, mass, summed = lax.map(run_stats, (segmented(query_heads, stride, segment),
                                                 segmented(key_heads, stride, segment),
                                                 segmented(value_heads, stride, segment)))
        peak_list.append(placed(peak, stride, NEGATIVE))
        mass_list.append(placed(mass, stride, 0.0))
        summed_list.append(placed(summed, stride, 0.0))
    peak_all = jnp.maximum(jnp.maximum(peak_list[0], peak_list[1]), peak_list[2])
    denom = jnp.zeros((total, H), jnp.float32)
    numer = jnp.zeros((total, H, E), jnp.float32)
    for branch in range(3):
        factor = jnp.exp(peak_list[branch] - peak_all)
        denom = denom + mass_list[branch] * factor
        numer = numer + summed_list[branch] * factor[..., None]
    position = jnp.arange(total)[:, None]
    head_ids = jnp.arange(H)[None, :]
    covered = ((position % R1 == head_ids % R1) | (position % R2 == head_ids % R2)
               | (position % R3 == head_ids % R3))
    safe = jnp.where(covered, denom, 1.0)
    result = jnp.where(covered[..., None], numer / safe[..., None], 0.0)
    log_total = peak_all + jnp.log(safe)
    dot_total = jnp.sum(grad_heads.astype(jnp.float32) * result, axis=-1)

    grad_q = jnp.zeros((total, H, E), jnp.float32)
    grad_k = jnp.zeros((total, H, E), jnp.float32)
    grad_v = jnp.zeros((total, H, E), jnp.float32)
    for stride, segment in configs:
        part_q, part_k, part_v = lax.map(run_grads, (segmented(query_heads, stride, segment),
                                                     segmented(key_heads, stride, segment),
                                                     segmented(value_heads, stride, segment),
                                                     segmented(grad_heads, stride, segment),
                                                     segmented(log_total, stride, segment),
                                                     segmented(dot_total, stride, segment)))
        grad_q = grad_q + placed(part_q, stride, 0.0)
        grad_k = grad_k + placed(part_k, stride, 0.0)
        grad_v = grad_v + placed(part_v, stride, 0.0)
    width = H * E
    return (result.reshape(total, width).astype(jnp.bfloat16), grad_q.reshape(total, width).astype(jnp.bfloat16),
            grad_k.reshape(total, width).astype(jnp.bfloat16), grad_v.reshape(total, width).astype(jnp.bfloat16))
```

```python
import functools

import jax
import jax.numpy as jnp
from jax import lax
from jax.experimental import pallas as pl
from jax.experimental.pallas import tpu as pltpu
from jax.sharding import PartitionSpec as P

E = 64
W1 = 512
R1 = 4
W2 = 8192
R2 = 64
KEYS = 512


NEGATIVE = -1e30


def product(form, left, right):
    return jnp.einsum(form, left, right, preferred_element_type=jnp.float32)


def pick(matrix, stride):
    length = matrix.shape[0]
    count = matrix.shape[1]
    folded = matrix.reshape((length // stride, stride) + matrix.shape[1:])
    return jnp.stack([folded[:, head % stride, head] for head in range(count)], axis=1)


def spread(matrix, stride, filler):
    count = matrix.shape[1]
    extra = (1,) * (matrix.ndim - 2)
    selector = (jnp.arange(stride)[:, None] == jnp.arange(count)[None, :] % stride).reshape(
        (1, stride, count) + extra
    )
    placed = jnp.where(selector, matrix[:, None], filler)
    return placed.reshape((matrix.shape[0] * stride,) + matrix.shape[1:])


def part_stats(query_sel, key_sel, value_sel):
    scale = query_sel.shape[-1] ** (-0.5)
    scores = product("qhe,khe->hqk", query_sel, key_sel) * scale
    peak = jnp.max(scores, axis=-1)
    weights = jnp.exp(scores - peak[..., None])
    mass = jnp.sum(weights, axis=-1)
    summed = product("hqk,khe->qhe", weights.astype(jnp.bfloat16), value_sel)
    return (peak.T, mass.T, summed)


def part_grads(query_sel, key_sel, value_sel, grad_sel, log_sel, dot_sel):
    scale = query_sel.shape[-1] ** (-0.5)
    scores = product("qhe,khe->hqk", query_sel, key_sel) * scale
    weights = jnp.exp(scores - log_sel.T[:, :, None])
    grad_v = product("hqk,qhe->khe", weights.astype(jnp.bfloat16), grad_sel)
    grad_w = product("qhe,khe->hqk", grad_sel, value_sel)
    grad_s = (weights * (grad_w - dot_sel.T[:, :, None]) * scale).astype(jnp.bfloat16)
    grad_q = product("hqk,khe->qhe", grad_s, key_sel)
    grad_k = product("hqk,qhe->khe", grad_s, query_sel)
    return (grad_q, grad_k, grad_v)


def run_stats(items):
    return part_stats(*items)


def run_grads(items):
    return part_grads(*items)


def general_shards(queries, key_rows, value_rows, grad_out):
    rows = queries.shape[0]
    width = queries.shape[1]
    heads = width // E
    devices_all = lax.axis_size("outer") * lax.axis_size("inner")
    stride_far = rows * devices_all // KEYS
    span = W2 // rows
    per_device = rows // R2
    near_count = rows // W1
    slide_pos = lax.axis_index(("outer", "inner"))
    query_heads = queries.reshape(rows, heads, E)
    key_heads = key_rows.reshape(rows, heads, E)
    value_heads = value_rows.reshape(rows, heads, E)
    grad_heads = grad_out.reshape(rows, heads, E)
    mid_pair = jnp.stack(
        [
            pick(key_heads, R2).reshape(per_device, width),
            pick(value_heads, R2).reshape(per_device, width),
        ]
    )
    far_pair = jnp.stack(
        [
            pick(key_heads, stride_far).reshape(-1, width),
            pick(value_heads, stride_far).reshape(-1, width),
        ]
    )
    first_row = slide_pos // span * (span * per_device)
    slide_mid, slide_far = (
        lax.all_gather(mid_pair, ("outer", "inner"), axis=1, tiled=True),
        lax.all_gather(far_pair, ("outer", "inner"), axis=1, tiled=True),
    )
    segment_pair = lax.dynamic_slice_in_dim(slide_mid, first_row, span * per_device, 1)
    key_mid = segment_pair[0].reshape(-1, heads, E)
    value_mid = segment_pair[1].reshape(-1, heads, E)
    key_far = slide_far[0].reshape(-1, heads, E)
    value_far = slide_far[1].reshape(-1, heads, E)

    def near_rows(matrix):
        return pick(matrix, R1).reshape((near_count, W1 // R1) + matrix.shape[1:])

    query_near = near_rows(query_heads)
    key_near = near_rows(key_heads)
    value_near = near_rows(value_heads)
    query_mid = pick(query_heads, R2)
    query_far = pick(query_heads, stride_far)
    peak_near, mass_near, summed_near = lax.map(run_stats, (query_near, key_near, value_near))
    peak_mid, mass_mid, summed_mid = part_stats(query_mid, key_mid, value_mid)
    peak_far, mass_far, summed_far = part_stats(query_far, key_far, value_far)
    branches = (
        (
            peak_near.reshape(-1, heads),
            mass_near.reshape(-1, heads),
            summed_near.reshape(-1, heads, E),
            R1,
        ),
        (peak_mid, mass_mid, summed_mid, R2),
        (peak_far, mass_far, summed_far, stride_far),
    )
    peak_list = [spread(item[0], item[3], NEGATIVE) for item in branches]
    peak_all = jnp.maximum(jnp.maximum(peak_list[0], peak_list[1]), peak_list[2])
    denom = jnp.zeros((rows, heads), jnp.float32)
    numer = jnp.zeros((rows, heads, E), jnp.float32)
    for branch in range(3):
        factor = jnp.exp(peak_list[branch] - peak_all)
        denom = denom + spread(branches[branch][1], branches[branch][3], 0.0) * factor
        numer = numer + spread(branches[branch][2], branches[branch][3], 0.0) * factor[..., None]
    position = jnp.arange(rows)[:, None]
    head_ids = jnp.arange(heads)[None, :]
    covered = (
        (position % R1 == head_ids % R1)
        | (position % R2 == head_ids % R2)
        | (position % stride_far == head_ids % stride_far)
    )
    safe = jnp.where(covered, denom, 1.0)
    result = jnp.where(covered[..., None], numer / safe[..., None], 0.0)
    log_total = peak_all + jnp.log(safe)
    dot_total = jnp.sum(grad_heads.astype(jnp.float32) * result, axis=-1)
    gq_near, gk_near, gv_near = lax.map(
        run_grads,
        (
            query_near,
            key_near,
            value_near,
            near_rows(grad_heads),
            near_rows(log_total),
            near_rows(dot_total),
        ),
    )
    gq_mid, gk_mid, gv_mid = part_grads(
        query_mid,
        key_mid,
        value_mid,
        pick(grad_heads, R2),
        pick(log_total, R2),
        pick(dot_total, R2),
    )
    gq_far, gk_far, gv_far = part_grads(
        query_far,
        key_far,
        value_far,
        pick(grad_heads, stride_far),
        pick(log_total, stride_far),
        pick(dot_total, stride_far),
    )
    mid_grads = jnp.stack([gk_mid.reshape(-1, width), gv_mid.reshape(-1, width)])
    far_grads = jnp.stack([gk_far.reshape(-1, width), gv_far.reshape(-1, width)])
    padded = jnp.zeros((2, devices_all * per_device, width), jnp.float32)
    padded = lax.dynamic_update_slice_in_dim(padded, mid_grads, first_row, 1)
    own_mid, own_far = (
        lax.psum_scatter(padded, ("outer", "inner"), scatter_dimension=1, tiled=True),
        lax.psum_scatter(far_grads, ("outer", "inner"), scatter_dimension=1, tiled=True),
    )
    grad_q = (
        spread(gq_near.reshape(-1, heads, E), R1, 0.0)
        + spread(gq_mid, R2, 0.0)
        + spread(gq_far, stride_far, 0.0)
    )
    grad_k = (
        spread(gk_near.reshape(-1, heads, E), R1, 0.0)
        + spread(own_mid[0].reshape(-1, heads, E), R2, 0.0)
        + spread(own_far[0].reshape(-1, heads, E), stride_far, 0.0)
    )
    grad_v = (
        spread(gv_near.reshape(-1, heads, E), R1, 0.0)
        + spread(own_mid[1].reshape(-1, heads, E), R2, 0.0)
        + spread(own_far[1].reshape(-1, heads, E), stride_far, 0.0)
    )
    return (
        result.reshape(rows, width).astype(jnp.bfloat16),
        grad_q.reshape(rows, width).astype(jnp.bfloat16),
        grad_k.reshape(rows, width).astype(jnp.bfloat16),
        grad_v.reshape(rows, width).astype(jnp.bfloat16),
    )


def dot_nt(left, right):
    return lax.dot_general(left, right, (((1,), (1,)), ((), ())), preferred_element_type=jnp.float32)


def dot_nn(left, right):
    return lax.dot_general(left, right, (((1,), (0,)), ((), ())), preferred_element_type=jnp.float32)


def dot_tn(left, right):
    return lax.dot_general(left, right, (((0,), (0,)), ((), ())), preferred_element_type=jnp.float32)


def chunk_offsets(head, stride):
    first = head % stride
    return [first] + [t for t in range(head % R1, stride, R1) if t != first]


def slide_kernel(
    devices, inner, heads, stride,
    q_ref, k_ref, v_ref, g_ref,
    out_ref, gq_ref, gk_ref, gv_ref,
    qf, kf, vf, gf, qg_near, kv_near, kv_far, part, recv,
    send_a, recv_a, send_b, recv_b,
):
    rows = q_ref.shape[0]
    far = rows // stride
    near = rows // R1
    pairs = heads // 2
    scale = E ** (-0.5)
    outer_id = lax.axis_index("outer")
    inner_id = lax.axis_index("inner")
    me = outer_id * inner + inner_id

    def target(peer):
        return {"outer": peer // inner, "inner": lax.rem(peer, inner)}

    def peer_of(step):
        return lax.rem(me + step, devices)

    barrier = pltpu.get_barrier_semaphore()

    def greet(step, carry):
        pl.semaphore_signal(
            barrier, inc=1, device_id=target(peer_of(step)), device_id_type=pl.DeviceIdType.MESH
        )
        return carry

    lax.fori_loop(1, devices, greet, 0)

    lane = lax.broadcasted_iota(jnp.int32, (far, 2 * E), 1)
    low = lane < E

    def swap(x):
        return pltpu.roll(x, E, 1)

    def joined(left_f, right_f, head, offset):
        a = left_f[head // 2, pl.ds(offset, far, stride=stride), :]
        b = right_f[head // 2, pl.ds(offset, far, stride=stride), :]
        if head % 2 == 0:
            return jnp.where(low, a, swap(b)).astype(jnp.bfloat16)
        return jnp.where(low, swap(a), b).astype(jnp.bfloat16)

    def widen(wide, ref):
        for pair in range(pairs):
            wide[pair] = ref[:, pl.ds(pair * 2 * E, 2 * E)].astype(jnp.float32)

    def narrow(ref, wide):
        for pair in range(pairs):
            ref[:, pl.ds(pair * 2 * E, 2 * E)] = wide[pair].astype(jnp.bfloat16)

    widen(kf, k_ref)
    widen(vf, v_ref)
    for head in range(heads):
        block = joined(kf, vf, head, chunk_offsets(head, stride)[0])
        kv_near[head, pl.ds(0, far), :] = block
        kv_far[me, head, :, :] = block

    pl.semaphore_wait(barrier, devices - 1)

    def gather_copy(step):
        peer = peer_of(step)
        return pltpu.make_async_remote_copy(
            src_ref=kv_far.at[me],
            dst_ref=kv_far.at[me],
            send_sem=send_a.at[step],
            recv_sem=recv_a.at[me],
            device_id=target(peer),
            device_id_type=pl.DeviceIdType.MESH,
        )

    def gather_arrival(step):
        peer = peer_of(step)
        return pltpu.make_async_remote_copy(
            src_ref=kv_far.at[peer],
            dst_ref=kv_far.at[peer],
            send_sem=send_a.at[step],
            recv_sem=recv_a.at[peer],
            device_id=target(peer),
            device_id_type=pl.DeviceIdType.MESH,
        )

    def run(fn):
        def body(step, carry):
            fn(step)
            return carry
        lax.fori_loop(1, devices, body, 0)

    run(lambda step: gather_copy(step).start())

    widen(qf, q_ref)
    widen(gf, g_ref)
    for head in range(heads):
        for index, offset in enumerate(chunk_offsets(head, stride)):
            span = pl.ds(index * far, far)
            if index:
                kv_near[head, span, :] = joined(kf, vf, head, offset)
            qg_near[head, span, :] = joined(qf, gf, head, offset)

    zeros = jnp.zeros((far, 2 * E), jnp.float32)
    for ref in (qf, kf, vf, gf):
        for pair in range(pairs):
            for offset in range(stride):
                if offset % R1 not in ((2 * pair) % R1, (2 * pair + 1) % R1):
                    ref[pair, pl.ds(offset, far, stride=stride), :] = zeros

    def split(qg):
        half = lax.broadcasted_iota(jnp.int32, qg.shape, 1) < E
        none = jnp.zeros_like(qg)
        return jnp.where(half, qg, none), jnp.where(half, none, qg)

    def attend(q_only, g_only, score_keys, counts):
        scores = jnp.concatenate([dot_nt(q_only, keys) for keys in score_keys], axis=1) * scale
        grad_w = jnp.concatenate([dot_nt(g_only, keys) for keys in score_keys], axis=1)
        peak = jnp.max(scores, axis=1, keepdims=True)
        weights = jnp.exp(scores - peak)
        if counts is not None:
            weights = weights * counts
        mass = jnp.sum(weights, axis=1, keepdims=True)
        inverse = 1.0 / mass
        rounded = weights.astype(jnp.bfloat16)
        summed, start = None, 0
        for keys in score_keys:
            term = dot_nn(rounded[:, start:start + keys.shape[0]], keys)
            summed = term if summed is None else summed + term
            start += keys.shape[0]
        result = summed * inverse
        dots = jnp.sum(g_only.astype(jnp.float32) * result, axis=1, keepdims=True)
        shares = weights * inverse
        grad_s = (shares * (grad_w - dots) * scale).astype(jnp.bfloat16)
        grad_q, start = None, 0
        for keys in score_keys:
            term = dot_nn(grad_s[:, start:start + keys.shape[0]], keys)
            grad_q = term if grad_q is None else grad_q + term
            start += keys.shape[0]
        both = jnp.concatenate([grad_s, shares.astype(jnp.bfloat16)], axis=0)
        grad_kv = dot_tn(both, jnp.concatenate([q_only, g_only], axis=0))
        return result, grad_q, grad_kv

    def place(ref, head, index, value, high):
        offset = chunk_offsets(head, stride)[index]
        odd = head % 2 == 1
        if odd != high:
            value = swap(value)
        kept = jnp.where(low, 0.0, value) if odd else jnp.where(low, value, 0.0)
        ref[head // 2, pl.ds(offset, far, stride=stride), :] = kept

    near_grads = []
    for head in range(heads):
        keys = kv_near[head]
        q_only, g_only = split(qg_near[head, pl.ds(far, near - far), :])
        result, grad_q, grad_kv = attend(q_only, g_only, [keys], None)
        for index in range(1, stride // R1):
            rows_in = slice((index - 1) * far, index * far)
            place(vf, head, index, result[rows_in], True)
            place(qf, head, index, grad_q[rows_in], False)
        near_grads.append(grad_kv)

    run(lambda step: gather_arrival(step).wait_recv())

    total = devices * far
    row_id = lax.broadcasted_iota(jnp.int32, (far, near + total), 0)
    col_id = lax.broadcasted_iota(jnp.int32, (far, near + total), 1)
    ratio = R2 // stride
    twice = (col_id >= near) & (row_id % ratio == 0) & ((col_id - near) % ratio == 0)
    counts = jnp.where(twice, 2.0, 1.0)
    for head in range(heads):
        keys = kv_near[head]
        far_keys = kv_far[:, head].reshape(total, 2 * E)
        q_only, g_only = split(qg_near[head, pl.ds(0, far), :])
        result, grad_q, grad_kv = attend(q_only, g_only, [keys, far_keys], counts)
        place(vf, head, 0, result, True)
        place(qf, head, 0, grad_q, False)
        near_grads[head] = near_grads[head] + grad_kv[:near]
        part[:, head] = grad_kv[near:].reshape(devices, far, 2 * E).astype(jnp.bfloat16)
    recv[me] = part[me]

    def scatter_copy(step):
        peer = peer_of(step)
        return pltpu.make_async_remote_copy(
            src_ref=part.at[peer],
            dst_ref=recv.at[me],
            send_sem=send_b.at[step],
            recv_sem=recv_b.at[me],
            device_id=target(peer),
            device_id_type=pl.DeviceIdType.MESH,
        )

    def scatter_arrival(step):
        peer = peer_of(step)
        return pltpu.make_async_remote_copy(
            src_ref=part.at[peer],
            dst_ref=recv.at[peer],
            send_sem=send_b.at[step],
            recv_sem=recv_b.at[peer],
            device_id=target(peer),
            device_id_type=pl.DeviceIdType.MESH,
        )

    run(lambda step: scatter_copy(step).start())
    narrow(out_ref, vf)
    narrow(gq_ref, qf)
    for head in range(heads):
        for index in range(1, stride // R1):
            piece = near_grads[head][index * far:(index + 1) * far]
            place(kf, head, index, piece, False)
            place(gf, head, index, piece, True)
    run(lambda step: scatter_arrival(step).wait_recv())
    for head in range(heads):
        piece = near_grads[head][:far] + jnp.sum(recv[:, head].astype(jnp.float32), axis=0)
        place(kf, head, 0, piece, False)
        place(gf, head, 0, piece, True)
    narrow(gk_ref, kf)
    narrow(gv_ref, gf)
    run(lambda step: gather_copy(step).wait_send())
    run(lambda step: scatter_copy(step).wait_send())


def slide_shards(queries, key_rows, value_rows, grad_out):
    rows, width = queries.shape
    heads = width // E
    inner = lax.axis_size("inner")
    devices = lax.axis_size("outer") * inner
    stride = rows * devices // KEYS
    far = rows // stride
    near = rows // R1
    whole = pl.BlockSpec(memory_space=pltpu.VMEM)
    return pl.pallas_call(
        functools.partial(slide_kernel, devices, inner, heads, stride),
        out_shape=[jax.ShapeDtypeStruct((rows, width), jnp.bfloat16)] * 4,
        in_specs=[whole] * 4,
        out_specs=[whole] * 4,
        scratch_shapes=[pltpu.VMEM((heads // 2, rows, 2 * E), jnp.float32)] * 4
        + [pltpu.VMEM((heads, near, 2 * E), jnp.bfloat16)] * 2
        + [pltpu.VMEM((devices, heads, far, 2 * E), jnp.bfloat16)] * 3
        + [pltpu.SemaphoreType.DMA((devices,))] * 4,
        compiler_params=pltpu.CompilerParams(
            collective_id=0, has_side_effects=True, vmem_limit_bytes=48 * 1024 * 1024
        ),
    )(queries, key_rows, value_rows, grad_out)


def shards(queries, key_rows, value_rows, grad_out):
    rows, width = queries.shape
    devices = lax.axis_size("outer") * lax.axis_size("inner")
    stride = rows * devices // KEYS
    one_segment = rows * devices == W2 and rows == W1 and (width // E) % 2 == 0
    nested = stride % R1 == 0 and R2 % stride == 0 and rows % (16 * stride) == 0
    if one_segment and nested and width // E <= stride:
        return slide_shards(queries, key_rows, value_rows, grad_out)
    return general_shards(queries, key_rows, value_rows, grad_out)


def solution(mesh):
    return jax.shard_map(
        shards,
        mesh=mesh,
        in_specs=(
            P(("group", "outer", "inner"), None),
            P(("group", "outer", "inner"), None),
            P(("group", "outer", "inner"), None),
            P(("group", "outer", "inner"), None),
        ),
        out_specs=(
            P(("group", "outer", "inner"), None),
            P(("group", "outer", "inner"), None),
            P(("group", "outer", "inner"), None),
            P(("group", "outer", "inner"), None),
        ),
        check_vma=False,
    )
```

```python
import functools

import jax
import jax.numpy as jnp
from jax import lax
from jax.experimental import pallas as pl
from jax.experimental.pallas import tpu as pltpu
from jax.sharding import PartitionSpec as P

E = 64
W1 = 512
R1 = 4
W2 = 8192
R2 = 64
KEYS = 512


NEGATIVE = -1e30


def product(form, left, right):
    return jnp.einsum(form, left, right, preferred_element_type=jnp.float32)


def pick(matrix, stride):
    length = matrix.shape[0]
    count = matrix.shape[1]
    folded = matrix.reshape((length // stride, stride) + matrix.shape[1:])
    return jnp.stack([folded[:, head % stride, head] for head in range(count)], axis=1)


def spread(matrix, stride, filler):
    count = matrix.shape[1]
    extra = (1,) * (matrix.ndim - 2)
    selector = (jnp.arange(stride)[:, None] == jnp.arange(count)[None, :] % stride).reshape(
        (1, stride, count) + extra
    )
    placed = jnp.where(selector, matrix[:, None], filler)
    return placed.reshape((matrix.shape[0] * stride,) + matrix.shape[1:])


def part_stats(query_sel, key_sel, value_sel):
    scale = query_sel.shape[-1] ** (-0.5)
    scores = product("qhe,khe->hqk", query_sel, key_sel) * scale
    peak = jnp.max(scores, axis=-1)
    weights = jnp.exp(scores - peak[..., None])
    mass = jnp.sum(weights, axis=-1)
    summed = product("hqk,khe->qhe", weights.astype(jnp.bfloat16), value_sel)
    return (peak.T, mass.T, summed)


def part_grads(query_sel, key_sel, value_sel, grad_sel, log_sel, dot_sel):
    scale = query_sel.shape[-1] ** (-0.5)
    scores = product("qhe,khe->hqk", query_sel, key_sel) * scale
    weights = jnp.exp(scores - log_sel.T[:, :, None])
    grad_v = product("hqk,qhe->khe", weights.astype(jnp.bfloat16), grad_sel)
    grad_w = product("qhe,khe->hqk", grad_sel, value_sel)
    grad_s = (weights * (grad_w - dot_sel.T[:, :, None]) * scale).astype(jnp.bfloat16)
    grad_q = product("hqk,khe->qhe", grad_s, key_sel)
    grad_k = product("hqk,qhe->khe", grad_s, query_sel)
    return (grad_q, grad_k, grad_v)


def run_stats(items):
    return part_stats(*items)


def run_grads(items):
    return part_grads(*items)


def general_shards(queries, key_rows, value_rows, grad_out):
    rows = queries.shape[0]
    width = queries.shape[1]
    heads = width // E
    devices_all = lax.axis_size("outer") * lax.axis_size("inner")
    stride_far = rows * devices_all // KEYS
    span = W2 // rows
    per_device = rows // R2
    near_count = rows // W1
    slide_pos = lax.axis_index(("outer", "inner"))
    query_heads = queries.reshape(rows, heads, E)
    key_heads = key_rows.reshape(rows, heads, E)
    value_heads = value_rows.reshape(rows, heads, E)
    grad_heads = grad_out.reshape(rows, heads, E)
    mid_pair = jnp.stack(
        [
            pick(key_heads, R2).reshape(per_device, width),
            pick(value_heads, R2).reshape(per_device, width),
        ]
    )
    far_pair = jnp.stack(
        [
            pick(key_heads, stride_far).reshape(-1, width),
            pick(value_heads, stride_far).reshape(-1, width),
        ]
    )
    first_row = slide_pos // span * (span * per_device)
    slide_mid, slide_far = (
        lax.all_gather(mid_pair, ("outer", "inner"), axis=1, tiled=True),
        lax.all_gather(far_pair, ("outer", "inner"), axis=1, tiled=True),
    )
    segment_pair = lax.dynamic_slice_in_dim(slide_mid, first_row, span * per_device, 1)
    key_mid = segment_pair[0].reshape(-1, heads, E)
    value_mid = segment_pair[1].reshape(-1, heads, E)
    key_far = slide_far[0].reshape(-1, heads, E)
    value_far = slide_far[1].reshape(-1, heads, E)

    def near_rows(matrix):
        return pick(matrix, R1).reshape((near_count, W1 // R1) + matrix.shape[1:])

    query_near = near_rows(query_heads)
    key_near = near_rows(key_heads)
    value_near = near_rows(value_heads)
    query_mid = pick(query_heads, R2)
    query_far = pick(query_heads, stride_far)
    peak_near, mass_near, summed_near = lax.map(run_stats, (query_near, key_near, value_near))
    peak_mid, mass_mid, summed_mid = part_stats(query_mid, key_mid, value_mid)
    peak_far, mass_far, summed_far = part_stats(query_far, key_far, value_far)
    branches = (
        (
            peak_near.reshape(-1, heads),
            mass_near.reshape(-1, heads),
            summed_near.reshape(-1, heads, E),
            R1,
        ),
        (peak_mid, mass_mid, summed_mid, R2),
        (peak_far, mass_far, summed_far, stride_far),
    )
    peak_list = [spread(item[0], item[3], NEGATIVE) for item in branches]
    peak_all = jnp.maximum(jnp.maximum(peak_list[0], peak_list[1]), peak_list[2])
    denom = jnp.zeros((rows, heads), jnp.float32)
    numer = jnp.zeros((rows, heads, E), jnp.float32)
    for branch in range(3):
        factor = jnp.exp(peak_list[branch] - peak_all)
        denom = denom + spread(branches[branch][1], branches[branch][3], 0.0) * factor
        numer = numer + spread(branches[branch][2], branches[branch][3], 0.0) * factor[..., None]
    position = jnp.arange(rows)[:, None]
    head_ids = jnp.arange(heads)[None, :]
    covered = (
        (position % R1 == head_ids % R1)
        | (position % R2 == head_ids % R2)
        | (position % stride_far == head_ids % stride_far)
    )
    safe = jnp.where(covered, denom, 1.0)
    result = jnp.where(covered[..., None], numer / safe[..., None], 0.0)
    log_total = peak_all + jnp.log(safe)
    dot_total = jnp.sum(grad_heads.astype(jnp.float32) * result, axis=-1)
    gq_near, gk_near, gv_near = lax.map(
        run_grads,
        (
            query_near,
            key_near,
            value_near,
            near_rows(grad_heads),
            near_rows(log_total),
            near_rows(dot_total),
        ),
    )
    gq_mid, gk_mid, gv_mid = part_grads(
        query_mid,
        key_mid,
        value_mid,
        pick(grad_heads, R2),
        pick(log_total, R2),
        pick(dot_total, R2),
    )
    gq_far, gk_far, gv_far = part_grads(
        query_far,
        key_far,
        value_far,
        pick(grad_heads, stride_far),
        pick(log_total, stride_far),
        pick(dot_total, stride_far),
    )
    mid_grads = jnp.stack([gk_mid.reshape(-1, width), gv_mid.reshape(-1, width)])
    far_grads = jnp.stack([gk_far.reshape(-1, width), gv_far.reshape(-1, width)])
    padded = jnp.zeros((2, devices_all * per_device, width), jnp.float32)
    padded = lax.dynamic_update_slice_in_dim(padded, mid_grads, first_row, 1)
    own_mid, own_far = (
        lax.psum_scatter(padded, ("outer", "inner"), scatter_dimension=1, tiled=True),
        lax.psum_scatter(far_grads, ("outer", "inner"), scatter_dimension=1, tiled=True),
    )
    grad_q = (
        spread(gq_near.reshape(-1, heads, E), R1, 0.0)
        + spread(gq_mid, R2, 0.0)
        + spread(gq_far, stride_far, 0.0)
    )
    grad_k = (
        spread(gk_near.reshape(-1, heads, E), R1, 0.0)
        + spread(own_mid[0].reshape(-1, heads, E), R2, 0.0)
        + spread(own_far[0].reshape(-1, heads, E), stride_far, 0.0)
    )
    grad_v = (
        spread(gv_near.reshape(-1, heads, E), R1, 0.0)
        + spread(own_mid[1].reshape(-1, heads, E), R2, 0.0)
        + spread(own_far[1].reshape(-1, heads, E), stride_far, 0.0)
    )
    return (
        result.reshape(rows, width).astype(jnp.bfloat16),
        grad_q.reshape(rows, width).astype(jnp.bfloat16),
        grad_k.reshape(rows, width).astype(jnp.bfloat16),
        grad_v.reshape(rows, width).astype(jnp.bfloat16),
    )


def dot_nt(left, right):
    return lax.dot_general(left, right, (((1,), (1,)), ((), ())), preferred_element_type=jnp.float32)


def dot_nn(left, right):
    return lax.dot_general(left, right, (((1,), (0,)), ((), ())), preferred_element_type=jnp.float32)


def dot_tn(left, right):
    return lax.dot_general(left, right, (((0,), (0,)), ((), ())), preferred_element_type=jnp.float32)


def chunk_offsets(head, stride):
    first = head % stride
    return [first] + [t for t in range(head % R1, stride, R1) if t != first]


def slide_kernel(
    inner, heads, stride,
    q_hbm, k_hbm, v_hbm, g_hbm,
    out_ref, gq_ref, gk_ref, gv_ref,
    q_ref, k_ref, v_ref, g_ref, load_sem,
    qf, kf, vf, gf, qg_near, kv_near, kv_far, part, from_core, by_x, from_x, by_z, from_z,
    send_a, recv_a, send_core, recv_core, send_x, recv_x, send_z, recv_z,
):
    loads = [
        pltpu.make_async_copy(source, target, load_sem.at[index])
        for index, (source, target) in enumerate(
            ((k_hbm, k_ref), (v_hbm, v_ref), (q_hbm, q_ref), (g_hbm, g_ref))
        )
    ]
    for load in loads:
        load.start()
    devices = 2 * inner
    zs = inner // 2
    groups = kv_far.shape[0]
    group_heads = heads // groups
    rows = q_ref.shape[0]
    far = rows // stride
    near = rows // R1
    pairs = heads // 2
    scale = E ** (-0.5)
    outer_id = lax.axis_index("outer")
    inner_id = lax.axis_index("inner")
    me = outer_id * inner + inner_id
    my_z = inner_id // 2
    my_x = lax.rem(inner_id, 2)
    MESH = pl.DeviceIdType.MESH
    to_core = {"outer": 1 - outer_id, "inner": inner_id}
    to_x = {"outer": outer_id, "inner": 2 * my_z + 1 - my_x}

    def peer_z(step):
        return lax.rem(my_z + step, zs)

    def to_z(step):
        return {"outer": outer_id, "inner": 2 * peer_z(step) + my_x}

    neighbours = [to_core, to_x] + [to_z(step) for step in range(1, zs)]
    barrier = pltpu.get_barrier_semaphore()
    for neighbour in neighbours:
        pl.semaphore_signal(barrier, inc=1, device_id=neighbour, device_id_type=MESH)

    lane = lax.broadcasted_iota(jnp.int32, (far, 2 * E), 1)
    low = lane < E

    def swap(x):
        return pltpu.roll(x, E, 1)

    def joined(left_f, right_f, head, offset):
        a = left_f[head // 2, pl.ds(offset, far, stride=stride), :]
        b = right_f[head // 2, pl.ds(offset, far, stride=stride), :]
        if head % 2 == 0:
            return jnp.where(low, a, swap(b)).astype(jnp.bfloat16)
        return jnp.where(low, swap(a), b).astype(jnp.bfloat16)

    def widen(wide, ref):
        for pair in range(pairs):
            wide[pair] = ref[:, pl.ds(pair * 2 * E, 2 * E)].astype(jnp.float32)

    def narrow(ref, wide):
        for pair in range(pairs):
            ref[:, pl.ds(pair * 2 * E, 2 * E)] = wide[pair].astype(jnp.bfloat16)

    loads[0].wait()
    widen(kf, k_ref)
    loads[1].wait()
    widen(vf, v_ref)
    for head in range(heads):
        block = joined(kf, vf, head, chunk_offsets(head, stride)[0])
        kv_near[head, pl.ds(0, far), :] = block
        kv_far[head // group_heads, me, head % group_heads] = block

    pl.semaphore_wait(barrier, len(neighbours))

    def block_id(core, z, x):
        return core * inner + 2 * z + x

    pending = []

    def send_block(group, block, slot, device):
        copy = pltpu.make_async_remote_copy(
            src_ref=kv_far.at[group, block],
            dst_ref=kv_far.at[group, block],
            send_sem=send_a.at[group, slot],
            recv_sem=recv_a.at[group, block],
            device_id=device,
            device_id_type=MESH,
        )
        copy.start()
        pending.append(copy)

    def await_block(group, block):
        pltpu.make_async_remote_copy(
            src_ref=kv_far.at[group, block],
            dst_ref=kv_far.at[group, block],
            send_sem=send_a.at[group, 0],
            recv_sem=recv_a.at[group, block],
            device_id=to_core,
            device_id_type=MESH,
        ).wait_recv()

    def send_own(group):
        for step in range(1, zs):
            send_block(group, me, step, to_z(step))
        send_block(group, me, zs, to_x)
        send_block(group, me, zs + 1, to_core)

    def pass_z(group):
        for step in range(1, zs):
            block = block_id(outer_id, peer_z(step), my_x)
            await_block(group, block)
            send_block(group, block, zs + 2 * step, to_x)
            send_block(group, block, zs + 2 * step + 1, to_core)

    def pass_x(group):
        for step in range(zs):
            block = block_id(outer_id, peer_z(step), 1 - my_x)
            await_block(group, block)
            send_block(group, block, 3 * zs + step, to_core)

    def finish_gather(group):
        for step in range(zs):
            for x in (my_x, 1 - my_x):
                await_block(group, block_id(1 - outer_id, peer_z(step), x))

    for group in range(groups):
        send_own(group)

    loads[2].wait()
    widen(qf, q_ref)
    loads[3].wait()
    widen(gf, g_ref)
    for head in range(heads):
        for index, offset in enumerate(chunk_offsets(head, stride)):
            span = pl.ds(index * far, far)
            if index:
                kv_near[head, span, :] = joined(kf, vf, head, offset)
            qg_near[head, span, :] = joined(qf, gf, head, offset)

    zeros = jnp.zeros((far, 2 * E), jnp.float32)
    for ref in (qf, kf, vf, gf):
        for pair in range(pairs):
            for offset in range(stride):
                if offset % R1 not in ((2 * pair) % R1, (2 * pair + 1) % R1):
                    ref[pair, pl.ds(offset, far, stride=stride), :] = zeros

    def split(qg):
        half = lax.broadcasted_iota(jnp.int32, qg.shape, 1) < E
        none = jnp.zeros_like(qg)
        return jnp.where(half, qg, none), jnp.where(half, none, qg)

    def attend(q_only, g_only, score_keys, counts):
        scores = jnp.concatenate([dot_nt(q_only, keys) for keys in score_keys], axis=1) * scale
        grad_w = jnp.concatenate([dot_nt(g_only, keys) for keys in score_keys], axis=1)
        peak = jnp.max(scores, axis=1, keepdims=True)
        weights = jnp.exp(scores - peak)
        if counts is not None:
            weights = weights * counts
        mass = jnp.sum(weights, axis=1, keepdims=True)
        inverse = 1.0 / mass
        rounded = weights.astype(jnp.bfloat16)
        summed, start = None, 0
        for keys in score_keys:
            term = dot_nn(rounded[:, start:start + keys.shape[0]], keys)
            summed = term if summed is None else summed + term
            start += keys.shape[0]
        result = summed * inverse
        dots = jnp.sum(g_only.astype(jnp.float32) * result, axis=1, keepdims=True)
        shares = weights * inverse
        grad_s = (shares * (grad_w - dots) * scale).astype(jnp.bfloat16)
        grad_q, start = None, 0
        for keys in score_keys:
            term = dot_nn(grad_s[:, start:start + keys.shape[0]], keys)
            grad_q = term if grad_q is None else grad_q + term
            start += keys.shape[0]
        both = jnp.concatenate([grad_s, shares.astype(jnp.bfloat16)], axis=0)
        grad_kv = dot_tn(both, jnp.concatenate([q_only, g_only], axis=0))
        return result, grad_q, grad_kv

    def place(ref, head, index, value, high):
        offset = chunk_offsets(head, stride)[index]
        odd = head % 2 == 1
        if odd != high:
            value = swap(value)
        kept = jnp.where(low, 0.0, value) if odd else jnp.where(low, value, 0.0)
        ref[head // 2, pl.ds(offset, far, stride=stride), :] = kept

    near_grads = []
    handing = [(pass_z, group) for group in range(groups)] + [(pass_x, group) for group in range(groups)]
    for head in range(heads):
        while len(handing) * heads > 2 * groups * (heads - 1 - head):
            step, group = handing.pop(0)
            step(group)
        keys = kv_near[head]
        q_only, g_only = split(qg_near[head, pl.ds(far, near - far), :])
        result, grad_q, grad_kv = attend(q_only, g_only, [keys], None)
        for index in range(1, stride // R1):
            rows_in = slice((index - 1) * far, index * far)
            place(vf, head, index, result[rows_in], True)
            place(qf, head, index, grad_q[rows_in], False)
        near_grads.append(grad_kv)

    total = devices * far
    row_id = lax.broadcasted_iota(jnp.int32, (far, near + total), 0)
    col_id = lax.broadcasted_iota(jnp.int32, (far, near + total), 1)
    ratio = R2 // stride
    twice = (col_id >= near) & (row_id % ratio == 0) & ((col_id - near) % ratio == 0)
    counts = jnp.where(twice, 2.0, 1.0)

    def core_copy(head):
        return pltpu.make_async_remote_copy(
            src_ref=part.at[head, 1 - outer_id],
            dst_ref=from_core.at[head],
            send_sem=send_core.at[head],
            recv_sem=recv_core.at[head],
            device_id=to_core,
            device_id_type=MESH,
        )

    def x_copy(head):
        return pltpu.make_async_remote_copy(
            src_ref=by_x.at[head, 1 - my_x],
            dst_ref=from_x.at[head],
            send_sem=send_x.at[head],
            recv_sem=recv_x.at[head],
            device_id=to_x,
            device_id_type=MESH,
        )

    def z_copy(head, step, slot):
        return pltpu.make_async_remote_copy(
            src_ref=by_z.at[head, peer_z(step)],
            dst_ref=from_z.at[head, slot],
            send_sem=send_z.at[head, step],
            recv_sem=recv_z.at[head, slot],
            device_id=to_z(step),
            device_id_type=MESH,
        )

    def reduce_core(head):
        core_copy(head).wait_recv()
        both = part[head, outer_id].astype(jnp.float32) + from_core[head].astype(jnp.float32)
        both = both.astype(jnp.bfloat16).reshape(zs, 2, far, 2 * E)
        for x in range(2):
            by_x[head, x] = both[:, x]
        x_copy(head).start()

    def reduce_x(head):
        x_copy(head).wait_recv()
        both = by_x[head, my_x].astype(jnp.float32) + from_x[head].astype(jnp.float32)
        by_z[head] = both.astype(jnp.bfloat16)
        for step in range(1, zs):
            z_copy(head, step, my_z).start()

    for head in range(heads):
        if head % group_heads == 0:
            finish_gather(head // group_heads)
        keys = kv_near[head]
        far_keys = kv_far[head // group_heads, :, head % group_heads].reshape(total, 2 * E)
        q_only, g_only = split(qg_near[head, pl.ds(0, far), :])
        result, grad_q, grad_kv = attend(q_only, g_only, [keys, far_keys], counts)
        place(vf, head, 0, result, True)
        place(qf, head, 0, grad_q, False)
        near_grads[head] = near_grads[head] + grad_kv[:near]
        part[head] = grad_kv[near:].reshape(2, inner, far, 2 * E).astype(jnp.bfloat16)
        core_copy(head).start()
        if head >= 1:
            reduce_core(head - 1)
        if head >= 2:
            reduce_x(head - 2)

    reduce_core(heads - 1)
    reduce_x(heads - 2)
    narrow(out_ref, vf)
    reduce_x(heads - 1)
    narrow(gq_ref, qf)
    for head in range(heads):
        for index in range(1, stride // R1):
            piece = near_grads[head][index * far:(index + 1) * far]
            place(kf, head, index, piece, False)
            place(gf, head, index, piece, True)
    for head in range(heads):
        piece = near_grads[head][:far] + by_z[head, my_z].astype(jnp.float32)
        for step in range(1, zs):
            z_copy(head, step, peer_z(step)).wait_recv()
            piece = piece + from_z[head, peer_z(step)].astype(jnp.float32)
        place(kf, head, 0, piece, False)
        place(gf, head, 0, piece, True)
    narrow(gk_ref, kf)
    narrow(gv_ref, gf)
    for copy in pending:
        copy.wait_send()
    for head in range(heads):
        core_copy(head).wait_send()
        x_copy(head).wait_send()
        for step in range(1, zs):
            z_copy(head, step, my_z).wait_send()


def slide_shards(queries, key_rows, value_rows, grad_out):
    rows, width = queries.shape
    heads = width // E
    inner = lax.axis_size("inner")
    devices = 2 * inner
    zs = inner // 2
    stride = rows * devices // KEYS
    far = rows // stride
    near = rows // R1
    groups = 2
    bf16 = jnp.bfloat16
    whole = pl.BlockSpec(memory_space=pltpu.VMEM)
    dma = pltpu.SemaphoreType.DMA
    return pl.pallas_call(
        functools.partial(slide_kernel, inner, heads, stride),
        out_shape=[jax.ShapeDtypeStruct((rows, width), bf16)] * 4,
        in_specs=[pl.BlockSpec(memory_space=pltpu.HBM)] * 4,
        out_specs=[whole] * 4,
        scratch_shapes=[pltpu.VMEM((rows, width), bf16)] * 4
        + [dma((4,))]
        + [pltpu.VMEM((heads // 2, rows, 2 * E), jnp.float32)] * 4
        + [pltpu.VMEM((heads, near, 2 * E), bf16)] * 2
        + [
            pltpu.VMEM((groups, devices, heads // groups, far, 2 * E), bf16),
            pltpu.VMEM((heads, 2, inner, far, 2 * E), bf16),
            pltpu.VMEM((heads, inner, far, 2 * E), bf16),
            pltpu.VMEM((heads, 2, zs, far, 2 * E), bf16),
            pltpu.VMEM((heads, zs, far, 2 * E), bf16),
            pltpu.VMEM((heads, zs, far, 2 * E), bf16),
            pltpu.VMEM((heads, zs, far, 2 * E), bf16),
            dma((groups, 4 * zs)),
            dma((groups, devices)),
            dma((heads,)),
            dma((heads,)),
            dma((heads,)),
            dma((heads,)),
            dma((heads, zs)),
            dma((heads, zs)),
        ],
        compiler_params=pltpu.CompilerParams(
            collective_id=0, has_side_effects=True, vmem_limit_bytes=63 * 1024 * 1024
        ),
    )(queries, key_rows, value_rows, grad_out)


def shards(queries, key_rows, value_rows, grad_out):
    rows, width = queries.shape
    devices = lax.axis_size("outer") * lax.axis_size("inner")
    stride = rows * devices // KEYS
    one_segment = rows * devices == W2 and rows == W1 and (width // E) % 2 == 0
    nested = stride % R1 == 0 and R2 % stride == 0 and rows % (16 * stride) == 0
    paired = lax.axis_size("outer") == 2 and lax.axis_size("inner") % 2 == 0
    if one_segment and nested and paired and width // E <= stride:
        return slide_shards(queries, key_rows, value_rows, grad_out)
    return general_shards(queries, key_rows, value_rows, grad_out)


def solution(mesh):
    return jax.shard_map(
        shards,
        mesh=mesh,
        in_specs=(
            P(("group", "outer", "inner"), None),
            P(("group", "outer", "inner"), None),
            P(("group", "outer", "inner"), None),
            P(("group", "outer", "inner"), None),
        ),
        out_specs=(
            P(("group", "outer", "inner"), None),
            P(("group", "outer", "inner"), None),
            P(("group", "outer", "inner"), None),
            P(("group", "outer", "inner"), None),
        ),
        check_vma=False,
    )
```

```python
import functools

import jax
import jax.numpy as jnp
from jax import lax
from jax.experimental import pallas as pl
from jax.experimental.pallas import tpu as pltpu
from jax.sharding import PartitionSpec as P

E = 64
W1 = 512
R1 = 4
W2 = 8192
R2 = 64
KEYS = 512


NEGATIVE = -1e30


def product(form, left, right):
    return jnp.einsum(form, left, right, preferred_element_type=jnp.float32)


def pick(matrix, stride):
    length = matrix.shape[0]
    count = matrix.shape[1]
    folded = matrix.reshape((length // stride, stride) + matrix.shape[1:])
    return jnp.stack([folded[:, head % stride, head] for head in range(count)], axis=1)


def spread(matrix, stride, filler):
    count = matrix.shape[1]
    extra = (1,) * (matrix.ndim - 2)
    selector = (jnp.arange(stride)[:, None] == jnp.arange(count)[None, :] % stride).reshape(
        (1, stride, count) + extra
    )
    placed = jnp.where(selector, matrix[:, None], filler)
    return placed.reshape((matrix.shape[0] * stride,) + matrix.shape[1:])


def part_stats(query_sel, key_sel, value_sel):
    scale = query_sel.shape[-1] ** (-0.5)
    scores = product("qhe,khe->hqk", query_sel, key_sel) * scale
    peak = jnp.max(scores, axis=-1)
    weights = jnp.exp(scores - peak[..., None])
    mass = jnp.sum(weights, axis=-1)
    summed = product("hqk,khe->qhe", weights.astype(jnp.bfloat16), value_sel)
    return (peak.T, mass.T, summed)


def part_grads(query_sel, key_sel, value_sel, grad_sel, log_sel, dot_sel):
    scale = query_sel.shape[-1] ** (-0.5)
    scores = product("qhe,khe->hqk", query_sel, key_sel) * scale
    weights = jnp.exp(scores - log_sel.T[:, :, None])
    grad_v = product("hqk,qhe->khe", weights.astype(jnp.bfloat16), grad_sel)
    grad_w = product("qhe,khe->hqk", grad_sel, value_sel)
    grad_s = (weights * (grad_w - dot_sel.T[:, :, None]) * scale).astype(jnp.bfloat16)
    grad_q = product("hqk,khe->qhe", grad_s, key_sel)
    grad_k = product("hqk,qhe->khe", grad_s, query_sel)
    return (grad_q, grad_k, grad_v)


def run_stats(items):
    return part_stats(*items)


def run_grads(items):
    return part_grads(*items)


def general_shards(queries, key_rows, value_rows, grad_out):
    rows = queries.shape[0]
    width = queries.shape[1]
    heads = width // E
    devices_all = lax.axis_size("outer") * lax.axis_size("inner")
    stride_far = rows * devices_all // KEYS
    span = W2 // rows
    per_device = rows // R2
    near_count = rows // W1
    slide_pos = lax.axis_index(("outer", "inner"))
    query_heads = queries.reshape(rows, heads, E)
    key_heads = key_rows.reshape(rows, heads, E)
    value_heads = value_rows.reshape(rows, heads, E)
    grad_heads = grad_out.reshape(rows, heads, E)
    mid_pair = jnp.stack(
        [
            pick(key_heads, R2).reshape(per_device, width),
            pick(value_heads, R2).reshape(per_device, width),
        ]
    )
    far_pair = jnp.stack(
        [
            pick(key_heads, stride_far).reshape(-1, width),
            pick(value_heads, stride_far).reshape(-1, width),
        ]
    )
    first_row = slide_pos // span * (span * per_device)
    slide_mid, slide_far = (
        lax.all_gather(mid_pair, ("outer", "inner"), axis=1, tiled=True),
        lax.all_gather(far_pair, ("outer", "inner"), axis=1, tiled=True),
    )
    segment_pair = lax.dynamic_slice_in_dim(slide_mid, first_row, span * per_device, 1)
    key_mid = segment_pair[0].reshape(-1, heads, E)
    value_mid = segment_pair[1].reshape(-1, heads, E)
    key_far = slide_far[0].reshape(-1, heads, E)
    value_far = slide_far[1].reshape(-1, heads, E)

    def near_rows(matrix):
        return pick(matrix, R1).reshape((near_count, W1 // R1) + matrix.shape[1:])

    query_near = near_rows(query_heads)
    key_near = near_rows(key_heads)
    value_near = near_rows(value_heads)
    query_mid = pick(query_heads, R2)
    query_far = pick(query_heads, stride_far)
    peak_near, mass_near, summed_near = lax.map(run_stats, (query_near, key_near, value_near))
    peak_mid, mass_mid, summed_mid = part_stats(query_mid, key_mid, value_mid)
    peak_far, mass_far, summed_far = part_stats(query_far, key_far, value_far)
    branches = (
        (
            peak_near.reshape(-1, heads),
            mass_near.reshape(-1, heads),
            summed_near.reshape(-1, heads, E),
            R1,
        ),
        (peak_mid, mass_mid, summed_mid, R2),
        (peak_far, mass_far, summed_far, stride_far),
    )
    peak_list = [spread(item[0], item[3], NEGATIVE) for item in branches]
    peak_all = jnp.maximum(jnp.maximum(peak_list[0], peak_list[1]), peak_list[2])
    denom = jnp.zeros((rows, heads), jnp.float32)
    numer = jnp.zeros((rows, heads, E), jnp.float32)
    for branch in range(3):
        factor = jnp.exp(peak_list[branch] - peak_all)
        denom = denom + spread(branches[branch][1], branches[branch][3], 0.0) * factor
        numer = numer + spread(branches[branch][2], branches[branch][3], 0.0) * factor[..., None]
    position = jnp.arange(rows)[:, None]
    head_ids = jnp.arange(heads)[None, :]
    covered = (
        (position % R1 == head_ids % R1)
        | (position % R2 == head_ids % R2)
        | (position % stride_far == head_ids % stride_far)
    )
    safe = jnp.where(covered, denom, 1.0)
    result = jnp.where(covered[..., None], numer / safe[..., None], 0.0)
    log_total = peak_all + jnp.log(safe)
    dot_total = jnp.sum(grad_heads.astype(jnp.float32) * result, axis=-1)
    gq_near, gk_near, gv_near = lax.map(
        run_grads,
        (
            query_near,
            key_near,
            value_near,
            near_rows(grad_heads),
            near_rows(log_total),
            near_rows(dot_total),
        ),
    )
    gq_mid, gk_mid, gv_mid = part_grads(
        query_mid,
        key_mid,
        value_mid,
        pick(grad_heads, R2),
        pick(log_total, R2),
        pick(dot_total, R2),
    )
    gq_far, gk_far, gv_far = part_grads(
        query_far,
        key_far,
        value_far,
        pick(grad_heads, stride_far),
        pick(log_total, stride_far),
        pick(dot_total, stride_far),
    )
    mid_grads = jnp.stack([gk_mid.reshape(-1, width), gv_mid.reshape(-1, width)])
    far_grads = jnp.stack([gk_far.reshape(-1, width), gv_far.reshape(-1, width)])
    padded = jnp.zeros((2, devices_all * per_device, width), jnp.float32)
    padded = lax.dynamic_update_slice_in_dim(padded, mid_grads, first_row, 1)
    own_mid, own_far = (
        lax.psum_scatter(padded, ("outer", "inner"), scatter_dimension=1, tiled=True),
        lax.psum_scatter(far_grads, ("outer", "inner"), scatter_dimension=1, tiled=True),
    )
    grad_q = (
        spread(gq_near.reshape(-1, heads, E), R1, 0.0)
        + spread(gq_mid, R2, 0.0)
        + spread(gq_far, stride_far, 0.0)
    )
    grad_k = (
        spread(gk_near.reshape(-1, heads, E), R1, 0.0)
        + spread(own_mid[0].reshape(-1, heads, E), R2, 0.0)
        + spread(own_far[0].reshape(-1, heads, E), stride_far, 0.0)
    )
    grad_v = (
        spread(gv_near.reshape(-1, heads, E), R1, 0.0)
        + spread(own_mid[1].reshape(-1, heads, E), R2, 0.0)
        + spread(own_far[1].reshape(-1, heads, E), stride_far, 0.0)
    )
    return (
        result.reshape(rows, width).astype(jnp.bfloat16),
        grad_q.reshape(rows, width).astype(jnp.bfloat16),
        grad_k.reshape(rows, width).astype(jnp.bfloat16),
        grad_v.reshape(rows, width).astype(jnp.bfloat16),
    )


def dot_nt(left, right):
    return lax.dot_general(left, right, (((1,), (1,)), ((), ())), preferred_element_type=jnp.float32)


def dot_nn(left, right):
    return lax.dot_general(left, right, (((1,), (0,)), ((), ())), preferred_element_type=jnp.float32)


def dot_tn(left, right):
    return lax.dot_general(left, right, (((0,), (0,)), ((), ())), preferred_element_type=jnp.float32)


def chunk_offsets(head, stride):
    first = head % stride
    return [first] + [t for t in range(head % R1, stride, R1) if t != first]


def slide_kernel(
    inner, heads, stride,
    q_hbm, k_hbm, v_hbm, g_hbm,
    out_ref, gq_ref, gk_ref, gv_ref,
    q_ref, k_ref, v_ref, g_ref, load_sem,
    qf, kf, vf, gf, qg_near, kv_near, kv_far, part, from_core, by_x, from_x, by_z, from_z,
    send_a, recv_a, send_core, recv_core, send_x, recv_x, send_z, recv_z,
):
    loads = [
        pltpu.make_async_copy(source, target, load_sem.at[index])
        for index, (source, target) in enumerate(
            ((k_hbm, k_ref), (v_hbm, v_ref), (q_hbm, q_ref), (g_hbm, g_ref))
        )
    ]
    for load in loads:
        load.start()
    lag = 3
    devices = 2 * inner
    zs = inner // 2
    groups = kv_far.shape[0]
    group_heads = heads // groups
    rows = q_ref.shape[0]
    far = rows // stride
    near = rows // R1
    pairs = heads // 2
    scale = E ** (-0.5)
    outer_id = lax.axis_index("outer")
    inner_id = lax.axis_index("inner")
    me = outer_id * inner + inner_id
    my_z = inner_id // 2
    my_x = lax.rem(inner_id, 2)
    MESH = pl.DeviceIdType.MESH
    to_core = {"outer": 1 - outer_id, "inner": inner_id}
    to_x = {"outer": outer_id, "inner": 2 * my_z + 1 - my_x}

    def peer_z(step):
        return lax.rem(my_z + step, zs)

    def to_z(step):
        return {"outer": outer_id, "inner": 2 * peer_z(step) + my_x}

    neighbours = [to_core, to_x] + [to_z(step) for step in range(1, zs)]
    barrier = pltpu.get_barrier_semaphore()
    for neighbour in neighbours:
        pl.semaphore_signal(barrier, inc=1, device_id=neighbour, device_id_type=MESH)

    lane = lax.broadcasted_iota(jnp.int32, (far, 2 * E), 1)
    low = lane < E

    def swap(x):
        return pltpu.roll(x, E, 1)

    def joined(left_f, right_f, head, offset):
        a = left_f[head // 2, pl.ds(offset, far, stride=stride), :]
        b = right_f[head // 2, pl.ds(offset, far, stride=stride), :]
        if head % 2 == 0:
            return jnp.where(low, a, swap(b)).astype(jnp.bfloat16)
        return jnp.where(low, swap(a), b).astype(jnp.bfloat16)

    def widen(wide, ref):
        for pair in range(pairs):
            wide[pair] = ref[:, pl.ds(pair * 2 * E, 2 * E)].astype(jnp.float32)

    def narrow(ref, wide):
        for pair in range(pairs):
            ref[:, pl.ds(pair * 2 * E, 2 * E)] = wide[pair].astype(jnp.bfloat16)

    loads[0].wait()
    widen(kf, k_ref)
    loads[1].wait()
    widen(vf, v_ref)
    for head in range(heads):
        block = joined(kf, vf, head, chunk_offsets(head, stride)[0])
        kv_near[head, pl.ds(0, far), :] = block
        kv_far[head // group_heads, me, head % group_heads] = block

    pl.semaphore_wait(barrier, len(neighbours))

    def block_id(core, z, x):
        return core * inner + 2 * z + x

    pending = []

    def send_block(group, block, slot, device):
        copy = pltpu.make_async_remote_copy(
            src_ref=kv_far.at[group, block],
            dst_ref=kv_far.at[group, block],
            send_sem=send_a.at[group, slot],
            recv_sem=recv_a.at[group, block],
            device_id=device,
            device_id_type=MESH,
        )
        copy.start()
        pending.append(copy)

    def await_block(group, block):
        pltpu.make_async_remote_copy(
            src_ref=kv_far.at[group, block],
            dst_ref=kv_far.at[group, block],
            send_sem=send_a.at[group, 0],
            recv_sem=recv_a.at[group, block],
            device_id=to_core,
            device_id_type=MESH,
        ).wait_recv()

    def send_own(group):
        for step in range(1, zs):
            send_block(group, me, step, to_z(step))
        send_block(group, me, zs, to_x)
        send_block(group, me, zs + 1, to_core)

    def pass_z(group):
        for step in range(1, zs):
            block = block_id(outer_id, peer_z(step), my_x)
            await_block(group, block)
            send_block(group, block, zs + 2 * step, to_x)
            send_block(group, block, zs + 2 * step + 1, to_core)

    def pass_x(group):
        for step in range(zs):
            block = block_id(outer_id, peer_z(step), 1 - my_x)
            await_block(group, block)
            send_block(group, block, 3 * zs + step, to_core)

    def finish_gather(group):
        for step in range(zs):
            for x in (my_x, 1 - my_x):
                await_block(group, block_id(1 - outer_id, peer_z(step), x))

    for group in range(groups):
        send_own(group)

    loads[2].wait()
    widen(qf, q_ref)
    loads[3].wait()
    widen(gf, g_ref)
    for head in range(heads):
        for index, offset in enumerate(chunk_offsets(head, stride)):
            span = pl.ds(index * far, far)
            if index:
                kv_near[head, span, :] = joined(kf, vf, head, offset)
            qg_near[head, span, :] = joined(qf, gf, head, offset)

    zeros = jnp.zeros((far, 2 * E), jnp.float32)
    for ref in (qf, kf, vf, gf):
        for pair in range(pairs):
            for offset in range(stride):
                if offset % R1 not in ((2 * pair) % R1, (2 * pair + 1) % R1):
                    ref[pair, pl.ds(offset, far, stride=stride), :] = zeros

    def split(qg):
        half = lax.broadcasted_iota(jnp.int32, qg.shape, 1) < E
        none = jnp.zeros_like(qg)
        return jnp.where(half, qg, none), jnp.where(half, none, qg)

    def attend(q_only, g_only, score_keys, counts):
        scores = jnp.concatenate([dot_nt(q_only, keys) for keys in score_keys], axis=1) * scale
        grad_w = jnp.concatenate([dot_nt(g_only, keys) for keys in score_keys], axis=1)
        peak = jnp.max(scores, axis=1, keepdims=True)
        weights = jnp.exp(scores - peak)
        if counts is not None:
            weights = weights * counts
        mass = jnp.sum(weights, axis=1, keepdims=True)
        inverse = 1.0 / mass
        rounded = weights.astype(jnp.bfloat16)
        summed, start = None, 0
        for keys in score_keys:
            term = dot_nn(rounded[:, start:start + keys.shape[0]], keys)
            summed = term if summed is None else summed + term
            start += keys.shape[0]
        result = summed * inverse
        dots = jnp.sum(g_only.astype(jnp.float32) * result, axis=1, keepdims=True)
        shares = weights * inverse
        grad_s = (shares * (grad_w - dots) * scale).astype(jnp.bfloat16)
        grad_q, start = None, 0
        for keys in score_keys:
            term = dot_nn(grad_s[:, start:start + keys.shape[0]], keys)
            grad_q = term if grad_q is None else grad_q + term
            start += keys.shape[0]
        both = jnp.concatenate([grad_s, shares.astype(jnp.bfloat16)], axis=0)
        grad_kv = dot_tn(both, jnp.concatenate([q_only, g_only], axis=0))
        return result, grad_q, grad_kv

    def place(ref, head, index, value, high):
        offset = chunk_offsets(head, stride)[index]
        odd = head % 2 == 1
        if odd != high:
            value = swap(value)
        kept = jnp.where(low, 0.0, value) if odd else jnp.where(low, value, 0.0)
        ref[head // 2, pl.ds(offset, far, stride=stride), :] = kept

    near_grads = []
    handing = [(pass_z, group) for group in range(groups)] + [(pass_x, group) for group in range(groups)]
    for head in range(heads):
        while len(handing) * heads > 2 * groups * (heads - 1 - head):
            step, group = handing.pop(0)
            step(group)
        keys = kv_near[head]
        q_only, g_only = split(qg_near[head, pl.ds(far, near - far), :])
        result, grad_q, grad_kv = attend(q_only, g_only, [keys], None)
        for index in range(1, stride // R1):
            rows_in = slice((index - 1) * far, index * far)
            place(vf, head, index, result[rows_in], True)
            place(qf, head, index, grad_q[rows_in], False)
        near_grads.append(grad_kv)

    total = devices * far
    row_id = lax.broadcasted_iota(jnp.int32, (far, near + total), 0)
    col_id = lax.broadcasted_iota(jnp.int32, (far, near + total), 1)
    ratio = R2 // stride
    twice = (col_id >= near) & (row_id % ratio == 0) & ((col_id - near) % ratio == 0)
    counts = jnp.where(twice, 2.0, 1.0)

    def core_copy(head):
        return pltpu.make_async_remote_copy(
            src_ref=part.at[head, 1 - outer_id],
            dst_ref=from_core.at[head],
            send_sem=send_core.at[head],
            recv_sem=recv_core.at[head],
            device_id=to_core,
            device_id_type=MESH,
        )

    def x_copy(head):
        return pltpu.make_async_remote_copy(
            src_ref=by_x.at[head, 1 - my_x],
            dst_ref=from_x.at[head],
            send_sem=send_x.at[head],
            recv_sem=recv_x.at[head],
            device_id=to_x,
            device_id_type=MESH,
        )

    def z_copy(head, step, slot):
        return pltpu.make_async_remote_copy(
            src_ref=by_z.at[head, peer_z(step)],
            dst_ref=from_z.at[head, slot],
            send_sem=send_z.at[head, step],
            recv_sem=recv_z.at[head, slot],
            device_id=to_z(step),
            device_id_type=MESH,
        )

    def reduce_core(head):
        core_copy(head).wait_recv()
        both = part[head, outer_id].astype(jnp.float32) + from_core[head].astype(jnp.float32)
        both = both.astype(jnp.bfloat16).reshape(zs, 2, far, 2 * E)
        for x in range(2):
            by_x[head, x] = both[:, x]
        x_copy(head).start()

    def reduce_x(head):
        x_copy(head).wait_recv()
        both = by_x[head, my_x].astype(jnp.float32) + from_x[head].astype(jnp.float32)
        by_z[head] = both.astype(jnp.bfloat16)
        for step in range(1, zs):
            z_copy(head, step, my_z).start()

    for head in range(heads):
        if head % group_heads == 0:
            finish_gather(head // group_heads)
        keys = kv_near[head]
        far_keys = kv_far[head // group_heads, :, head % group_heads].reshape(total, 2 * E)
        q_only, g_only = split(qg_near[head, pl.ds(0, far), :])
        result, grad_q, grad_kv = attend(q_only, g_only, [keys, far_keys], counts)
        place(vf, head, 0, result, True)
        place(qf, head, 0, grad_q, False)
        near_grads[head] = near_grads[head] + grad_kv[:near]
        part[head] = grad_kv[near:].reshape(2, inner, far, 2 * E).astype(jnp.bfloat16)
        core_copy(head).start()
        if head >= lag:
            reduce_core(head - lag)

    for head in range(heads - lag, heads):
        reduce_core(head)
    narrow(out_ref, vf)
    for head in range(heads):
        reduce_x(head)
        for index in range(1, stride // R1):
            piece = near_grads[head][index * far:(index + 1) * far]
            place(kf, head, index, piece, False)
            place(gf, head, index, piece, True)
    narrow(gq_ref, qf)
    for head in range(heads):
        piece = near_grads[head][:far] + by_z[head, my_z].astype(jnp.float32)
        for step in range(1, zs):
            z_copy(head, step, peer_z(step)).wait_recv()
            piece = piece + from_z[head, peer_z(step)].astype(jnp.float32)
        place(kf, head, 0, piece, False)
        place(gf, head, 0, piece, True)
    narrow(gk_ref, kf)
    narrow(gv_ref, gf)
    for copy in pending:
        copy.wait_send()
    for head in range(heads):
        core_copy(head).wait_send()
        x_copy(head).wait_send()
        for step in range(1, zs):
            z_copy(head, step, my_z).wait_send()


def store_kernel(*refs):
    sources, targets, sems = refs[:4], refs[4:8], refs[8]
    copies = [
        pltpu.make_async_copy(source, target, sems.at[index])
        for index, (source, target) in enumerate(zip(sources, targets))
    ]
    for copy in copies:
        copy.start()
    for copy in copies:
        copy.wait()


def slide_shards(queries, key_rows, value_rows, grad_out):
    rows, width = queries.shape
    heads = width // E
    inner = lax.axis_size("inner")
    devices = 2 * inner
    zs = inner // 2
    stride = rows * devices // KEYS
    far = rows // stride
    near = rows // R1
    groups = 2
    bf16 = jnp.bfloat16
    whole = pl.BlockSpec(memory_space=pltpu.VMEM)
    dma = pltpu.SemaphoreType.DMA
    results = pl.pallas_call(
        functools.partial(slide_kernel, inner, heads, stride),
        out_shape=[jax.ShapeDtypeStruct((rows, width), bf16)] * 4,
        in_specs=[pl.BlockSpec(memory_space=pltpu.HBM)] * 4,
        out_specs=[whole] * 4,
        scratch_shapes=[pltpu.VMEM((rows, width), bf16)] * 4
        + [dma((4,))]
        + [pltpu.VMEM((heads // 2, rows, 2 * E), jnp.float32)] * 4
        + [pltpu.VMEM((heads, near, 2 * E), bf16)] * 2
        + [
            pltpu.VMEM((groups, devices, heads // groups, far, 2 * E), bf16),
            pltpu.VMEM((heads, 2, inner, far, 2 * E), bf16),
            pltpu.VMEM((heads, inner, far, 2 * E), bf16),
            pltpu.VMEM((heads, 2, zs, far, 2 * E), bf16),
            pltpu.VMEM((heads, zs, far, 2 * E), bf16),
            pltpu.VMEM((heads, zs, far, 2 * E), bf16),
            pltpu.VMEM((heads, zs, far, 2 * E), bf16),
            dma((groups, 4 * zs)),
            dma((groups, devices)),
            dma((heads,)),
            dma((heads,)),
            dma((heads,)),
            dma((heads,)),
            dma((heads, zs)),
            dma((heads, zs)),
        ],
        compiler_params=pltpu.CompilerParams(
            collective_id=0, has_side_effects=True, vmem_limit_bytes=63 * 1024 * 1024
        ),
    )(queries, key_rows, value_rows, grad_out)
    return pl.pallas_call(
        store_kernel,
        out_shape=[jax.ShapeDtypeStruct((rows, width), bf16)] * 4,
        in_specs=[whole] * 4,
        out_specs=[pl.BlockSpec(memory_space=pltpu.HBM)] * 4,
        scratch_shapes=[dma((4,))],
    )(*results)


def shards(queries, key_rows, value_rows, grad_out):
    rows, width = queries.shape
    devices = lax.axis_size("outer") * lax.axis_size("inner")
    stride = rows * devices // KEYS
    one_segment = rows * devices == W2 and rows == W1 and (width // E) % 2 == 0
    nested = stride % R1 == 0 and R2 % stride == 0 and rows % (16 * stride) == 0
    paired = lax.axis_size("outer") == 2 and lax.axis_size("inner") % 2 == 0
    if one_segment and nested and paired and width // E <= stride:
        return slide_shards(queries, key_rows, value_rows, grad_out)
    return general_shards(queries, key_rows, value_rows, grad_out)


def solution(mesh):
    return jax.shard_map(
        shards,
        mesh=mesh,
        in_specs=(
            P(("group", "outer", "inner"), None),
            P(("group", "outer", "inner"), None),
            P(("group", "outer", "inner"), None),
            P(("group", "outer", "inner"), None),
        ),
        out_specs=(
            P(("group", "outer", "inner"), None),
            P(("group", "outer", "inner"), None),
            P(("group", "outer", "inner"), None),
            P(("group", "outer", "inner"), None),
        ),
        check_vma=False,
    )
```

```python
import functools

import jax
import jax.numpy as jnp
from jax import lax
from jax.experimental import pallas as pl
from jax.experimental.pallas import tpu as pltpu
from jax.sharding import PartitionSpec as P

E = 64
W1 = 512
R1 = 4
W2 = 8192
R2 = 64
KEYS = 512


NEGATIVE = -1e30


def product(form, left, right):
    return jnp.einsum(form, left, right, preferred_element_type=jnp.float32)


def pick(matrix, stride):
    length = matrix.shape[0]
    count = matrix.shape[1]
    folded = matrix.reshape((length // stride, stride) + matrix.shape[1:])
    return jnp.stack([folded[:, head % stride, head] for head in range(count)], axis=1)


def spread(matrix, stride, filler):
    count = matrix.shape[1]
    extra = (1,) * (matrix.ndim - 2)
    selector = (jnp.arange(stride)[:, None] == jnp.arange(count)[None, :] % stride).reshape(
        (1, stride, count) + extra
    )
    placed = jnp.where(selector, matrix[:, None], filler)
    return placed.reshape((matrix.shape[0] * stride,) + matrix.shape[1:])


def part_stats(query_sel, key_sel, value_sel):
    scale = query_sel.shape[-1] ** (-0.5)
    scores = product("qhe,khe->hqk", query_sel, key_sel) * scale
    peak = jnp.max(scores, axis=-1)
    weights = jnp.exp(scores - peak[..., None])
    mass = jnp.sum(weights, axis=-1)
    summed = product("hqk,khe->qhe", weights.astype(jnp.bfloat16), value_sel)
    return (peak.T, mass.T, summed)


def part_grads(query_sel, key_sel, value_sel, grad_sel, log_sel, dot_sel):
    scale = query_sel.shape[-1] ** (-0.5)
    scores = product("qhe,khe->hqk", query_sel, key_sel) * scale
    weights = jnp.exp(scores - log_sel.T[:, :, None])
    grad_v = product("hqk,qhe->khe", weights.astype(jnp.bfloat16), grad_sel)
    grad_w = product("qhe,khe->hqk", grad_sel, value_sel)
    grad_s = (weights * (grad_w - dot_sel.T[:, :, None]) * scale).astype(jnp.bfloat16)
    grad_q = product("hqk,khe->qhe", grad_s, key_sel)
    grad_k = product("hqk,qhe->khe", grad_s, query_sel)
    return (grad_q, grad_k, grad_v)


def run_stats(items):
    return part_stats(*items)


def run_grads(items):
    return part_grads(*items)


def general_shards(queries, key_rows, value_rows, grad_out):
    rows = queries.shape[0]
    width = queries.shape[1]
    heads = width // E
    devices_all = lax.axis_size("outer") * lax.axis_size("inner")
    stride_far = rows * devices_all // KEYS
    span = W2 // rows
    per_device = rows // R2
    near_count = rows // W1
    slide_pos = lax.axis_index(("outer", "inner"))
    query_heads = queries.reshape(rows, heads, E)
    key_heads = key_rows.reshape(rows, heads, E)
    value_heads = value_rows.reshape(rows, heads, E)
    grad_heads = grad_out.reshape(rows, heads, E)
    mid_pair = jnp.stack(
        [
            pick(key_heads, R2).reshape(per_device, width),
            pick(value_heads, R2).reshape(per_device, width),
        ]
    )
    far_pair = jnp.stack(
        [
            pick(key_heads, stride_far).reshape(-1, width),
            pick(value_heads, stride_far).reshape(-1, width),
        ]
    )
    first_row = slide_pos // span * (span * per_device)
    slide_mid, slide_far = (
        lax.all_gather(mid_pair, ("outer", "inner"), axis=1, tiled=True),
        lax.all_gather(far_pair, ("outer", "inner"), axis=1, tiled=True),
    )
    segment_pair = lax.dynamic_slice_in_dim(slide_mid, first_row, span * per_device, 1)
    key_mid = segment_pair[0].reshape(-1, heads, E)
    value_mid = segment_pair[1].reshape(-1, heads, E)
    key_far = slide_far[0].reshape(-1, heads, E)
    value_far = slide_far[1].reshape(-1, heads, E)

    def near_rows(matrix):
        return pick(matrix, R1).reshape((near_count, W1 // R1) + matrix.shape[1:])

    query_near = near_rows(query_heads)
    key_near = near_rows(key_heads)
    value_near = near_rows(value_heads)
    query_mid = pick(query_heads, R2)
    query_far = pick(query_heads, stride_far)
    peak_near, mass_near, summed_near = lax.map(run_stats, (query_near, key_near, value_near))
    peak_mid, mass_mid, summed_mid = part_stats(query_mid, key_mid, value_mid)
    peak_far, mass_far, summed_far = part_stats(query_far, key_far, value_far)
    branches = (
        (
            peak_near.reshape(-1, heads),
            mass_near.reshape(-1, heads),
            summed_near.reshape(-1, heads, E),
            R1,
        ),
        (peak_mid, mass_mid, summed_mid, R2),
        (peak_far, mass_far, summed_far, stride_far),
    )
    peak_list = [spread(item[0], item[3], NEGATIVE) for item in branches]
    peak_all = jnp.maximum(jnp.maximum(peak_list[0], peak_list[1]), peak_list[2])
    denom = jnp.zeros((rows, heads), jnp.float32)
    numer = jnp.zeros((rows, heads, E), jnp.float32)
    for branch in range(3):
        factor = jnp.exp(peak_list[branch] - peak_all)
        denom = denom + spread(branches[branch][1], branches[branch][3], 0.0) * factor
        numer = numer + spread(branches[branch][2], branches[branch][3], 0.0) * factor[..., None]
    position = jnp.arange(rows)[:, None]
    head_ids = jnp.arange(heads)[None, :]
    covered = (
        (position % R1 == head_ids % R1)
        | (position % R2 == head_ids % R2)
        | (position % stride_far == head_ids % stride_far)
    )
    safe = jnp.where(covered, denom, 1.0)
    result = jnp.where(covered[..., None], numer / safe[..., None], 0.0)
    log_total = peak_all + jnp.log(safe)
    dot_total = jnp.sum(grad_heads.astype(jnp.float32) * result, axis=-1)
    gq_near, gk_near, gv_near = lax.map(
        run_grads,
        (
            query_near,
            key_near,
            value_near,
            near_rows(grad_heads),
            near_rows(log_total),
            near_rows(dot_total),
        ),
    )
    gq_mid, gk_mid, gv_mid = part_grads(
        query_mid,
        key_mid,
        value_mid,
        pick(grad_heads, R2),
        pick(log_total, R2),
        pick(dot_total, R2),
    )
    gq_far, gk_far, gv_far = part_grads(
        query_far,
        key_far,
        value_far,
        pick(grad_heads, stride_far),
        pick(log_total, stride_far),
        pick(dot_total, stride_far),
    )
    mid_grads = jnp.stack([gk_mid.reshape(-1, width), gv_mid.reshape(-1, width)])
    far_grads = jnp.stack([gk_far.reshape(-1, width), gv_far.reshape(-1, width)])
    padded = jnp.zeros((2, devices_all * per_device, width), jnp.float32)
    padded = lax.dynamic_update_slice_in_dim(padded, mid_grads, first_row, 1)
    own_mid, own_far = (
        lax.psum_scatter(padded, ("outer", "inner"), scatter_dimension=1, tiled=True),
        lax.psum_scatter(far_grads, ("outer", "inner"), scatter_dimension=1, tiled=True),
    )
    grad_q = (
        spread(gq_near.reshape(-1, heads, E), R1, 0.0)
        + spread(gq_mid, R2, 0.0)
        + spread(gq_far, stride_far, 0.0)
    )
    grad_k = (
        spread(gk_near.reshape(-1, heads, E), R1, 0.0)
        + spread(own_mid[0].reshape(-1, heads, E), R2, 0.0)
        + spread(own_far[0].reshape(-1, heads, E), stride_far, 0.0)
    )
    grad_v = (
        spread(gv_near.reshape(-1, heads, E), R1, 0.0)
        + spread(own_mid[1].reshape(-1, heads, E), R2, 0.0)
        + spread(own_far[1].reshape(-1, heads, E), stride_far, 0.0)
    )
    return (
        result.reshape(rows, width).astype(jnp.bfloat16),
        grad_q.reshape(rows, width).astype(jnp.bfloat16),
        grad_k.reshape(rows, width).astype(jnp.bfloat16),
        grad_v.reshape(rows, width).astype(jnp.bfloat16),
    )


def dot_nt(left, right):
    return lax.dot_general(left, right, (((1,), (1,)), ((), ())), preferred_element_type=jnp.float32)


def dot_nn(left, right):
    return lax.dot_general(left, right, (((1,), (0,)), ((), ())), preferred_element_type=jnp.float32)


def dot_tn(left, right):
    return lax.dot_general(left, right, (((0,), (0,)), ((), ())), preferred_element_type=jnp.float32)


def chunk_offsets(head, stride):
    first = head % stride
    return [first] + [t for t in range(head % R1, stride, R1) if t != first]


def slide_kernel(
    inner, heads, stride,
    q_hbm, k_hbm, v_hbm, g_hbm,
    out_ref, gq_ref, gk_ref, gv_ref,
    q_ref, k_ref, v_ref, g_ref, load_sem,
    qf, kf, vf, gf, qg_near, kv_near, kv_far, part, from_core, by_x, from_x, by_z, from_z,
    send_a, recv_a, send_core, recv_core, send_x, recv_x, send_z, recv_z,
):
    loads = [
        pltpu.make_async_copy(source, target, load_sem.at[index])
        for index, (source, target) in enumerate(
            ((k_hbm, k_ref), (v_hbm, v_ref), (q_hbm, q_ref), (g_hbm, g_ref))
        )
    ]
    for load in loads:
        load.start()
    lag = 1
    early = 0
    bundles, batch = part.shape[0], part.shape[2]
    devices = 2 * inner
    zs = inner // 2
    groups = kv_far.shape[0]
    group_heads = heads // groups
    rows = q_ref.shape[0]
    far = rows // stride
    near = rows // R1
    pairs = heads // 2
    scale = E ** (-0.5)
    outer_id = lax.axis_index("outer")
    inner_id = lax.axis_index("inner")
    me = outer_id * inner + inner_id
    my_z = inner_id // 2
    my_x = lax.rem(inner_id, 2)
    MESH = pl.DeviceIdType.MESH
    to_core = {"outer": 1 - outer_id, "inner": inner_id}
    to_x = {"outer": outer_id, "inner": 2 * my_z + 1 - my_x}

    def peer_z(step):
        return lax.rem(my_z + step, zs)

    def to_z(step):
        return {"outer": outer_id, "inner": 2 * peer_z(step) + my_x}

    neighbours = [to_core, to_x] + [to_z(step) for step in range(1, zs)]
    barrier = pltpu.get_barrier_semaphore()
    for neighbour in neighbours:
        pl.semaphore_signal(barrier, inc=1, device_id=neighbour, device_id_type=MESH)

    lane = lax.broadcasted_iota(jnp.int32, (far, 2 * E), 1)
    low = lane < E

    def swap(x):
        return pltpu.roll(x, E, 1)

    def joined(left_f, right_f, head, offset):
        a = left_f[head // 2, pl.ds(offset, far, stride=stride), :]
        b = right_f[head // 2, pl.ds(offset, far, stride=stride), :]
        if head % 2 == 0:
            return jnp.where(low, a, swap(b)).astype(jnp.bfloat16)
        return jnp.where(low, swap(a), b).astype(jnp.bfloat16)

    def widen(wide, ref):
        for pair in range(pairs):
            wide[pair] = ref[:, pl.ds(pair * 2 * E, 2 * E)].astype(jnp.float32)

    def narrow(ref, wide):
        for pair in range(pairs):
            ref[:, pl.ds(pair * 2 * E, 2 * E)] = wide[pair].astype(jnp.bfloat16)

    loads[0].wait()
    widen(kf, k_ref)
    loads[1].wait()
    widen(vf, v_ref)
    for head in range(heads):
        block = joined(kf, vf, head, chunk_offsets(head, stride)[0])
        kv_near[head, pl.ds(0, far), :] = block
        kv_far[head // group_heads, me, head % group_heads] = block

    def block_id(core, z, x):
        return core * inner + 2 * z + x

    pending = []

    def send_block(group, block, slot, device):
        copy = pltpu.make_async_remote_copy(
            src_ref=kv_far.at[group, block],
            dst_ref=kv_far.at[group, block],
            send_sem=send_a.at[group, slot],
            recv_sem=recv_a.at[group, block],
            device_id=device,
            device_id_type=MESH,
        )
        copy.start()
        pending.append(copy)

    def await_block(group, block):
        pltpu.make_async_remote_copy(
            src_ref=kv_far.at[group, block],
            dst_ref=kv_far.at[group, block],
            send_sem=send_a.at[group, 0],
            recv_sem=recv_a.at[group, block],
            device_id=to_core,
            device_id_type=MESH,
        ).wait_recv()

    def send_own(group):
        for step in range(1, zs):
            send_block(group, me, step, to_z(step))
        send_block(group, me, zs, to_x)
        send_block(group, me, zs + 1, to_core)

    def pass_z(group):
        for step in range(1, zs):
            block = block_id(outer_id, peer_z(step), my_x)
            await_block(group, block)
            send_block(group, block, zs + 2 * step, to_x)
            send_block(group, block, zs + 2 * step + 1, to_core)

    def pass_x(group):
        for step in range(zs):
            block = block_id(outer_id, peer_z(step), 1 - my_x)
            await_block(group, block)
            send_block(group, block, 3 * zs + step, to_core)

    def finish_gather(group):
        for step in range(zs):
            for x in (my_x, 1 - my_x):
                await_block(group, block_id(1 - outer_id, peer_z(step), x))

    loads[2].wait()
    widen(qf, q_ref)
    loads[3].wait()
    widen(gf, g_ref)
    for head in range(heads):
        for index, offset in enumerate(chunk_offsets(head, stride)):
            span = pl.ds(index * far, far)
            if index:
                kv_near[head, span, :] = joined(kf, vf, head, offset)
            qg_near[head, span, :] = joined(qf, gf, head, offset)

    zeros = jnp.zeros((far, 2 * E), jnp.float32)
    for ref in (qf, kf, vf, gf):
        for pair in range(pairs):
            for offset in range(stride):
                if offset % R1 not in ((2 * pair) % R1, (2 * pair + 1) % R1):
                    ref[pair, pl.ds(offset, far, stride=stride), :] = zeros

    def split(qg):
        half = lax.broadcasted_iota(jnp.int32, qg.shape, 1) < E
        none = jnp.zeros_like(qg)
        return jnp.where(half, qg, none), jnp.where(half, none, qg)

    def attend(q_only, g_only, score_keys, counts):
        scores = jnp.concatenate([dot_nt(q_only, keys) for keys in score_keys], axis=1) * scale
        grad_w = jnp.concatenate([dot_nt(g_only, keys) for keys in score_keys], axis=1)
        peak = jnp.max(scores, axis=1, keepdims=True)
        weights = jnp.exp(scores - peak)
        if counts is not None:
            weights = weights * counts
        mass = jnp.sum(weights, axis=1, keepdims=True)
        inverse = 1.0 / mass
        rounded = weights.astype(jnp.bfloat16)
        summed, start = None, 0
        for keys in score_keys:
            term = dot_nn(rounded[:, start:start + keys.shape[0]], keys)
            summed = term if summed is None else summed + term
            start += keys.shape[0]
        result = summed * inverse
        dots = jnp.sum(g_only.astype(jnp.float32) * result, axis=1, keepdims=True)
        shares = weights * inverse
        grad_s = (shares * (grad_w - dots) * scale).astype(jnp.bfloat16)
        grad_q, start = None, 0
        for keys in score_keys:
            term = dot_nn(grad_s[:, start:start + keys.shape[0]], keys)
            grad_q = term if grad_q is None else grad_q + term
            start += keys.shape[0]
        both = jnp.concatenate([grad_s, shares.astype(jnp.bfloat16)], axis=0)
        grad_kv = dot_tn(both, jnp.concatenate([q_only, g_only], axis=0))
        return result, grad_q, grad_kv

    def place(ref, head, index, value, high):
        offset = chunk_offsets(head, stride)[index]
        odd = head % 2 == 1
        if odd != high:
            value = swap(value)
        kept = jnp.where(low, 0.0, value) if odd else jnp.where(low, value, 0.0)
        ref[head // 2, pl.ds(offset, far, stride=stride), :] = kept

    near_grads = []

    def near_head(head):
        keys = kv_near[head]
        q_only, g_only = split(qg_near[head, pl.ds(far, near - far), :])
        result, grad_q, grad_kv = attend(q_only, g_only, [keys], None)
        for index in range(1, stride // R1):
            rows_in = slice((index - 1) * far, index * far)
            place(vf, head, index, result[rows_in], True)
            place(qf, head, index, grad_q[rows_in], False)
        near_grads.append(grad_kv)

    for head in range(early):
        near_head(head)
    pl.semaphore_wait(barrier, len(neighbours))
    for group in range(groups):
        send_own(group)
    handing = [(pass_z, group) for group in range(groups)] + [(pass_x, group) for group in range(groups)]
    late = heads - early
    for head in range(late):
        near_head(early + head)
        while len(handing) * late > 2 * groups * (late - 1 - head):
            step, group = handing.pop(0)
            step(group)
    for step, group in handing:
        step(group)

    total = devices * far
    row_id = lax.broadcasted_iota(jnp.int32, (far, near + total), 0)
    col_id = lax.broadcasted_iota(jnp.int32, (far, near + total), 1)
    ratio = R2 // stride
    twice = (col_id >= near) & (row_id % ratio == 0) & ((col_id - near) % ratio == 0)
    counts = jnp.where(twice, 2.0, 1.0)

    def core_copy(bundle):
        return pltpu.make_async_remote_copy(
            src_ref=part.at[bundle, 1 - outer_id],
            dst_ref=from_core.at[bundle],
            send_sem=send_core.at[bundle],
            recv_sem=recv_core.at[bundle],
            device_id=to_core,
            device_id_type=MESH,
        )

    def x_copy(bundle):
        return pltpu.make_async_remote_copy(
            src_ref=by_x.at[bundle, 1 - my_x],
            dst_ref=from_x.at[bundle],
            send_sem=send_x.at[bundle],
            recv_sem=recv_x.at[bundle],
            device_id=to_x,
            device_id_type=MESH,
        )

    def z_copy(bundle, step, slot):
        return pltpu.make_async_remote_copy(
            src_ref=by_z.at[bundle, peer_z(step)],
            dst_ref=from_z.at[bundle, slot],
            send_sem=send_z.at[bundle, step],
            recv_sem=recv_z.at[bundle, slot],
            device_id=to_z(step),
            device_id_type=MESH,
        )

    def reduce_core(bundle):
        core_copy(bundle).wait_recv()
        both = part[bundle, outer_id].astype(jnp.float32) + from_core[bundle].astype(jnp.float32)
        both = both.astype(jnp.bfloat16).reshape(batch, zs, 2, far, 2 * E)
        for x in range(2):
            by_x[bundle, x] = both[:, :, x]
        x_copy(bundle).start()

    def reduce_x(bundle):
        x_copy(bundle).wait_recv()
        both = by_x[bundle, my_x].astype(jnp.float32) + from_x[bundle].astype(jnp.float32)
        both = both.astype(jnp.bfloat16)
        for inside in range(batch):
            by_z[bundle, :, inside] = both[inside]
        for step in range(1, zs):
            z_copy(bundle, step, my_z).start()

    for head in range(heads):
        if head % group_heads == 0:
            finish_gather(head // group_heads)
        keys = kv_near[head]
        far_keys = kv_far[head // group_heads, :, head % group_heads].reshape(total, 2 * E)
        q_only, g_only = split(qg_near[head, pl.ds(0, far), :])
        result, grad_q, grad_kv = attend(q_only, g_only, [keys, far_keys], counts)
        place(vf, head, 0, result, True)
        place(qf, head, 0, grad_q, False)
        near_grads[head] = near_grads[head] + grad_kv[:near]
        part[head // batch, :, head % batch] = (
            grad_kv[near:].reshape(2, inner, far, 2 * E).astype(jnp.bfloat16)
        )
        if head % batch == batch - 1:
            core_copy(head // batch).start()
            if head // batch >= lag:
                reduce_core(head // batch - lag)

    for bundle in range(max(0, bundles - lag), bundles):
        reduce_core(bundle)
    narrow(out_ref, vf)
    for head in range(heads):
        if head % batch == 0:
            reduce_x(head // batch)
        for index in range(1, stride // R1):
            piece = near_grads[head][index * far:(index + 1) * far]
            place(kf, head, index, piece, False)
            place(gf, head, index, piece, True)
    narrow(gq_ref, qf)
    for head in range(heads):
        bundle, inside = head // batch, head % batch
        piece = near_grads[head][:far] + by_z[bundle, my_z, inside].astype(jnp.float32)
        for step in range(1, zs):
            if inside == 0:
                z_copy(bundle, step, peer_z(step)).wait_recv()
            piece = piece + from_z[bundle, peer_z(step), inside].astype(jnp.float32)
        place(kf, head, 0, piece, False)
        place(gf, head, 0, piece, True)
    narrow(gk_ref, kf)
    narrow(gv_ref, gf)
    for copy in pending:
        copy.wait_send()
    for bundle in range(bundles):
        core_copy(bundle).wait_send()
        x_copy(bundle).wait_send()
        for step in range(1, zs):
            z_copy(bundle, step, my_z).wait_send()


def store_kernel(*refs):
    sources, targets, sems = refs[:4], refs[4:8], refs[8]
    copies = [
        pltpu.make_async_copy(source, target, sems.at[index])
        for index, (source, target) in enumerate(zip(sources, targets))
    ]
    for copy in copies:
        copy.start()
    for copy in copies:
        copy.wait()


def slide_shards(queries, key_rows, value_rows, grad_out):
    rows, width = queries.shape
    heads = width // E
    inner = lax.axis_size("inner")
    devices = 2 * inner
    zs = inner // 2
    stride = rows * devices // KEYS
    far = rows // stride
    near = rows // R1
    groups = 3
    batch = 2
    bundles = heads // batch
    bf16 = jnp.bfloat16
    whole = pl.BlockSpec(memory_space=pltpu.VMEM)
    dma = pltpu.SemaphoreType.DMA
    results = pl.pallas_call(
        functools.partial(slide_kernel, inner, heads, stride),
        out_shape=[jax.ShapeDtypeStruct((rows, width), bf16)] * 4,
        in_specs=[pl.BlockSpec(memory_space=pltpu.HBM)] * 4,
        out_specs=[whole] * 4,
        scratch_shapes=[pltpu.VMEM((rows, width), bf16)] * 4
        + [dma((4,))]
        + [pltpu.VMEM((heads // 2, rows, 2 * E), jnp.float32)] * 4
        + [pltpu.VMEM((heads, near, 2 * E), bf16)] * 2
        + [
            pltpu.VMEM((groups, devices, heads // groups, far, 2 * E), bf16),
            pltpu.VMEM((bundles, 2, batch, inner, far, 2 * E), bf16),
            pltpu.VMEM((bundles, batch, inner, far, 2 * E), bf16),
            pltpu.VMEM((bundles, 2, batch, zs, far, 2 * E), bf16),
            pltpu.VMEM((bundles, batch, zs, far, 2 * E), bf16),
            pltpu.VMEM((bundles, zs, batch, far, 2 * E), bf16),
            pltpu.VMEM((bundles, zs, batch, far, 2 * E), bf16),
            dma((groups, 4 * zs)),
            dma((groups, devices)),
            dma((bundles,)),
            dma((bundles,)),
            dma((bundles,)),
            dma((bundles,)),
            dma((bundles, zs)),
            dma((bundles, zs)),
        ],
        compiler_params=pltpu.CompilerParams(
            collective_id=0, has_side_effects=True, vmem_limit_bytes=63 * 1024 * 1024
        ),
    )(queries, key_rows, value_rows, grad_out)
    return pl.pallas_call(
        store_kernel,
        out_shape=[jax.ShapeDtypeStruct((rows, width), bf16)] * 4,
        in_specs=[whole] * 4,
        out_specs=[pl.BlockSpec(memory_space=pltpu.HBM)] * 4,
        scratch_shapes=[dma((4,))],
    )(*results)


def shards(queries, key_rows, value_rows, grad_out):
    rows, width = queries.shape
    devices = lax.axis_size("outer") * lax.axis_size("inner")
    stride = rows * devices // KEYS
    one_segment = rows * devices == W2 and rows == W1 and (width // E) % 2 == 0
    nested = stride % R1 == 0 and R2 % stride == 0 and rows % (16 * stride) == 0
    paired = lax.axis_size("outer") == 2 and lax.axis_size("inner") % 2 == 0
    if one_segment and nested and paired and width // E <= stride:
        return slide_shards(queries, key_rows, value_rows, grad_out)
    return general_shards(queries, key_rows, value_rows, grad_out)


def solution(mesh):
    return jax.shard_map(
        shards,
        mesh=mesh,
        in_specs=(
            P(("group", "outer", "inner"), None),
            P(("group", "outer", "inner"), None),
            P(("group", "outer", "inner"), None),
            P(("group", "outer", "inner"), None),
        ),
        out_specs=(
            P(("group", "outer", "inner"), None),
            P(("group", "outer", "inner"), None),
            P(("group", "outer", "inner"), None),
            P(("group", "outer", "inner"), None),
        ),
        check_vma=False,
    )
```

```python
import functools

import jax
import jax.numpy as jnp
from jax import lax
from jax.experimental import pallas as pl
from jax.experimental.pallas import tpu as pltpu
from jax.sharding import PartitionSpec as P

E = 64
W1 = 512
R1 = 4
W2 = 8192
R2 = 64
KEYS = 512


NEGATIVE = -1e30


def product(form, left, right):
    return jnp.einsum(form, left, right, preferred_element_type=jnp.float32)


def pick(matrix, stride):
    length = matrix.shape[0]
    count = matrix.shape[1]
    folded = matrix.reshape((length // stride, stride) + matrix.shape[1:])
    return jnp.stack([folded[:, head % stride, head] for head in range(count)], axis=1)


def spread(matrix, stride, filler):
    count = matrix.shape[1]
    extra = (1,) * (matrix.ndim - 2)
    selector = (jnp.arange(stride)[:, None] == jnp.arange(count)[None, :] % stride).reshape(
        (1, stride, count) + extra
    )
    placed = jnp.where(selector, matrix[:, None], filler)
    return placed.reshape((matrix.shape[0] * stride,) + matrix.shape[1:])


def part_stats(query_sel, key_sel, value_sel):
    scale = query_sel.shape[-1] ** (-0.5)
    scores = product("qhe,khe->hqk", query_sel, key_sel) * scale
    peak = jnp.max(scores, axis=-1)
    weights = jnp.exp(scores - peak[..., None])
    mass = jnp.sum(weights, axis=-1)
    summed = product("hqk,khe->qhe", weights.astype(jnp.bfloat16), value_sel)
    return (peak.T, mass.T, summed)


def part_grads(query_sel, key_sel, value_sel, grad_sel, log_sel, dot_sel):
    scale = query_sel.shape[-1] ** (-0.5)
    scores = product("qhe,khe->hqk", query_sel, key_sel) * scale
    weights = jnp.exp(scores - log_sel.T[:, :, None])
    grad_v = product("hqk,qhe->khe", weights.astype(jnp.bfloat16), grad_sel)
    grad_w = product("qhe,khe->hqk", grad_sel, value_sel)
    grad_s = (weights * (grad_w - dot_sel.T[:, :, None]) * scale).astype(jnp.bfloat16)
    grad_q = product("hqk,khe->qhe", grad_s, key_sel)
    grad_k = product("hqk,qhe->khe", grad_s, query_sel)
    return (grad_q, grad_k, grad_v)


def run_stats(items):
    return part_stats(*items)


def run_grads(items):
    return part_grads(*items)


def general_shards(queries, key_rows, value_rows, grad_out):
    rows = queries.shape[0]
    width = queries.shape[1]
    heads = width // E
    devices_all = lax.axis_size("outer") * lax.axis_size("inner")
    stride_far = rows * devices_all // KEYS
    span = W2 // rows
    per_device = rows // R2
    near_count = rows // W1
    slide_pos = lax.axis_index(("outer", "inner"))
    query_heads = queries.reshape(rows, heads, E)
    key_heads = key_rows.reshape(rows, heads, E)
    value_heads = value_rows.reshape(rows, heads, E)
    grad_heads = grad_out.reshape(rows, heads, E)
    mid_pair = jnp.stack(
        [
            pick(key_heads, R2).reshape(per_device, width),
            pick(value_heads, R2).reshape(per_device, width),
        ]
    )
    far_pair = jnp.stack(
        [
            pick(key_heads, stride_far).reshape(-1, width),
            pick(value_heads, stride_far).reshape(-1, width),
        ]
    )
    first_row = slide_pos // span * (span * per_device)
    slide_mid, slide_far = (
        lax.all_gather(mid_pair, ("outer", "inner"), axis=1, tiled=True),
        lax.all_gather(far_pair, ("outer", "inner"), axis=1, tiled=True),
    )
    segment_pair = lax.dynamic_slice_in_dim(slide_mid, first_row, span * per_device, 1)
    key_mid = segment_pair[0].reshape(-1, heads, E)
    value_mid = segment_pair[1].reshape(-1, heads, E)
    key_far = slide_far[0].reshape(-1, heads, E)
    value_far = slide_far[1].reshape(-1, heads, E)

    def near_rows(matrix):
        return pick(matrix, R1).reshape((near_count, W1 // R1) + matrix.shape[1:])

    query_near = near_rows(query_heads)
    key_near = near_rows(key_heads)
    value_near = near_rows(value_heads)
    query_mid = pick(query_heads, R2)
    query_far = pick(query_heads, stride_far)
    peak_near, mass_near, summed_near = lax.map(run_stats, (query_near, key_near, value_near))
    peak_mid, mass_mid, summed_mid = part_stats(query_mid, key_mid, value_mid)
    peak_far, mass_far, summed_far = part_stats(query_far, key_far, value_far)
    branches = (
        (
            peak_near.reshape(-1, heads),
            mass_near.reshape(-1, heads),
            summed_near.reshape(-1, heads, E),
            R1,
        ),
        (peak_mid, mass_mid, summed_mid, R2),
        (peak_far, mass_far, summed_far, stride_far),
    )
    peak_list = [spread(item[0], item[3], NEGATIVE) for item in branches]
    peak_all = jnp.maximum(jnp.maximum(peak_list[0], peak_list[1]), peak_list[2])
    denom = jnp.zeros((rows, heads), jnp.float32)
    numer = jnp.zeros((rows, heads, E), jnp.float32)
    for branch in range(3):
        factor = jnp.exp(peak_list[branch] - peak_all)
        denom = denom + spread(branches[branch][1], branches[branch][3], 0.0) * factor
        numer = numer + spread(branches[branch][2], branches[branch][3], 0.0) * factor[..., None]
    position = jnp.arange(rows)[:, None]
    head_ids = jnp.arange(heads)[None, :]
    covered = (
        (position % R1 == head_ids % R1)
        | (position % R2 == head_ids % R2)
        | (position % stride_far == head_ids % stride_far)
    )
    safe = jnp.where(covered, denom, 1.0)
    result = jnp.where(covered[..., None], numer / safe[..., None], 0.0)
    log_total = peak_all + jnp.log(safe)
    dot_total = jnp.sum(grad_heads.astype(jnp.float32) * result, axis=-1)
    gq_near, gk_near, gv_near = lax.map(
        run_grads,
        (
            query_near,
            key_near,
            value_near,
            near_rows(grad_heads),
            near_rows(log_total),
            near_rows(dot_total),
        ),
    )
    gq_mid, gk_mid, gv_mid = part_grads(
        query_mid,
        key_mid,
        value_mid,
        pick(grad_heads, R2),
        pick(log_total, R2),
        pick(dot_total, R2),
    )
    gq_far, gk_far, gv_far = part_grads(
        query_far,
        key_far,
        value_far,
        pick(grad_heads, stride_far),
        pick(log_total, stride_far),
        pick(dot_total, stride_far),
    )
    mid_grads = jnp.stack([gk_mid.reshape(-1, width), gv_mid.reshape(-1, width)])
    far_grads = jnp.stack([gk_far.reshape(-1, width), gv_far.reshape(-1, width)])
    padded = jnp.zeros((2, devices_all * per_device, width), jnp.float32)
    padded = lax.dynamic_update_slice_in_dim(padded, mid_grads, first_row, 1)
    own_mid, own_far = (
        lax.psum_scatter(padded, ("outer", "inner"), scatter_dimension=1, tiled=True),
        lax.psum_scatter(far_grads, ("outer", "inner"), scatter_dimension=1, tiled=True),
    )
    grad_q = (
        spread(gq_near.reshape(-1, heads, E), R1, 0.0)
        + spread(gq_mid, R2, 0.0)
        + spread(gq_far, stride_far, 0.0)
    )
    grad_k = (
        spread(gk_near.reshape(-1, heads, E), R1, 0.0)
        + spread(own_mid[0].reshape(-1, heads, E), R2, 0.0)
        + spread(own_far[0].reshape(-1, heads, E), stride_far, 0.0)
    )
    grad_v = (
        spread(gv_near.reshape(-1, heads, E), R1, 0.0)
        + spread(own_mid[1].reshape(-1, heads, E), R2, 0.0)
        + spread(own_far[1].reshape(-1, heads, E), stride_far, 0.0)
    )
    return (
        result.reshape(rows, width).astype(jnp.bfloat16),
        grad_q.reshape(rows, width).astype(jnp.bfloat16),
        grad_k.reshape(rows, width).astype(jnp.bfloat16),
        grad_v.reshape(rows, width).astype(jnp.bfloat16),
    )


def dot_nt(left, right):
    return lax.dot_general(left, right, (((1,), (1,)), ((), ())), preferred_element_type=jnp.float32)


def dot_nn(left, right):
    return lax.dot_general(left, right, (((1,), (0,)), ((), ())), preferred_element_type=jnp.float32)


def dot_tn(left, right):
    return lax.dot_general(left, right, (((0,), (0,)), ((), ())), preferred_element_type=jnp.float32)


def chunk_offsets(head, stride):
    first = head % stride
    return [first] + [t for t in range(head % R1, stride, R1) if t != first]


def slide_kernel(
    inner, heads, stride,
    q_hbm, k_hbm, v_hbm, g_hbm,
    out_ref, gq_ref, gk_ref, gv_ref,
    q_ref, k_ref, v_ref, g_ref, load_sem,
    qf, kf, vf, gf, qg_near, kv_near, kv_far, part, from_core, by_x, from_x, by_z, from_z,
    send_a, recv_a, send_core, recv_core, send_x, recv_x, send_z, recv_z,
):
    loads = [
        pltpu.make_async_copy(source, target, load_sem.at[index])
        for index, (source, target) in enumerate(
            ((k_hbm, k_ref), (v_hbm, v_ref), (q_hbm, q_ref), (g_hbm, g_ref))
        )
    ]
    for load in loads:
        load.start()
    lag = 1
    early = 0
    bundles, batch = part.shape[0], part.shape[2]
    devices = 2 * inner
    zs = inner // 2
    groups = kv_far.shape[0]
    group_heads = heads // groups
    rows = q_ref.shape[0]
    far = rows // stride
    near = rows // R1
    pairs = heads // 2
    scale = E ** (-0.5)
    outer_id = lax.axis_index("outer")
    inner_id = lax.axis_index("inner")
    me = outer_id * inner + inner_id
    my_z = inner_id // 2
    my_x = lax.rem(inner_id, 2)
    MESH = pl.DeviceIdType.MESH
    to_core = {"outer": 1 - outer_id, "inner": inner_id}
    to_x = {"outer": outer_id, "inner": 2 * my_z + 1 - my_x}

    def peer_z(step):
        return lax.rem(my_z + step, zs)

    def to_z(step):
        return {"outer": outer_id, "inner": 2 * peer_z(step) + my_x}

    neighbours = [to_core, to_x] + [to_z(step) for step in range(1, zs)]
    barrier = pltpu.get_barrier_semaphore()
    for neighbour in neighbours:
        pl.semaphore_signal(barrier, inc=1, device_id=neighbour, device_id_type=MESH)

    lane = lax.broadcasted_iota(jnp.int32, (far, 2 * E), 1)
    low = lane < E

    def swap(x):
        return pltpu.roll(x, E, 1)

    def joined(left_f, right_f, head, offset):
        a = left_f[head // 2, pl.ds(offset, far, stride=stride), :]
        b = right_f[head // 2, pl.ds(offset, far, stride=stride), :]
        if head % 2 == 0:
            return jnp.where(low, a, swap(b)).astype(jnp.bfloat16)
        return jnp.where(low, swap(a), b).astype(jnp.bfloat16)

    def widen(wide, ref):
        for pair in range(pairs):
            wide[pair] = ref[:, pl.ds(pair * 2 * E, 2 * E)].astype(jnp.float32)

    def narrow_pair(ref, wide, pair):
        ref[:, pl.ds(pair * 2 * E, 2 * E)] = wide[pair].astype(jnp.bfloat16)

    def narrow(ref, wide):
        for pair in range(pairs):
            narrow_pair(ref, wide, pair)

    loads[0].wait()
    widen(kf, k_ref)
    loads[1].wait()
    widen(vf, v_ref)
    for head in range(heads):
        block = joined(kf, vf, head, chunk_offsets(head, stride)[0])
        kv_near[head, pl.ds(0, far), :] = block
        kv_far[head // group_heads, me, head % group_heads] = block

    def block_id(core, z, x):
        return core * inner + 2 * z + x

    pending = []

    def send_block(group, block, slot, device):
        copy = pltpu.make_async_remote_copy(
            src_ref=kv_far.at[group, block],
            dst_ref=kv_far.at[group, block],
            send_sem=send_a.at[group, slot],
            recv_sem=recv_a.at[group, block],
            device_id=device,
            device_id_type=MESH,
        )
        copy.start()
        pending.append(copy)

    def await_block(group, block):
        pltpu.make_async_remote_copy(
            src_ref=kv_far.at[group, block],
            dst_ref=kv_far.at[group, block],
            send_sem=send_a.at[group, 0],
            recv_sem=recv_a.at[group, block],
            device_id=to_core,
            device_id_type=MESH,
        ).wait_recv()

    def send_own(group):
        for step in range(1, zs):
            send_block(group, me, step, to_z(step))
        send_block(group, me, zs, to_x)
        send_block(group, me, zs + 1, to_core)

    def pass_z(group):
        for step in range(1, zs):
            block = block_id(outer_id, peer_z(step), my_x)
            await_block(group, block)
            send_block(group, block, zs + 2 * step, to_x)
            send_block(group, block, zs + 2 * step + 1, to_core)

    def pass_x(group):
        for step in range(zs):
            block = block_id(outer_id, peer_z(step), 1 - my_x)
            await_block(group, block)
            send_block(group, block, 3 * zs + step, to_core)

    def finish_gather(group):
        for step in range(zs):
            for x in (my_x, 1 - my_x):
                await_block(group, block_id(1 - outer_id, peer_z(step), x))

    loads[2].wait()
    widen(qf, q_ref)
    loads[3].wait()
    widen(gf, g_ref)
    for head in range(heads):
        for index, offset in enumerate(chunk_offsets(head, stride)):
            span = pl.ds(index * far, far)
            if index:
                kv_near[head, span, :] = joined(kf, vf, head, offset)
            qg_near[head, span, :] = joined(qf, gf, head, offset)

    zeros = jnp.zeros((far, 2 * E), jnp.float32)
    for ref in (qf, kf, vf, gf):
        for pair in range(pairs):
            for offset in range(stride):
                if offset % R1 not in ((2 * pair) % R1, (2 * pair + 1) % R1):
                    ref[pair, pl.ds(offset, far, stride=stride), :] = zeros

    def split(qg):
        half = lax.broadcasted_iota(jnp.int32, qg.shape, 1) < E
        none = jnp.zeros_like(qg)
        return jnp.where(half, qg, none), jnp.where(half, none, qg)

    def attend(q_only, g_only, score_keys, counts):
        scores = jnp.concatenate([dot_nt(q_only, keys) for keys in score_keys], axis=1) * scale
        grad_w = jnp.concatenate([dot_nt(g_only, keys) for keys in score_keys], axis=1)
        peak = jnp.max(scores, axis=1, keepdims=True)
        weights = jnp.exp(scores - peak)
        if counts is not None:
            weights = weights * counts
        mass = jnp.sum(weights, axis=1, keepdims=True)
        inverse = 1.0 / mass
        rounded = weights.astype(jnp.bfloat16)
        summed, start = None, 0
        for keys in score_keys:
            term = dot_nn(rounded[:, start:start + keys.shape[0]], keys)
            summed = term if summed is None else summed + term
            start += keys.shape[0]
        result = summed * inverse
        dots = jnp.sum(g_only.astype(jnp.float32) * result, axis=1, keepdims=True)
        shares = weights * inverse
        grad_s = (shares * (grad_w - dots) * scale).astype(jnp.bfloat16)
        grad_q, start = None, 0
        for keys in score_keys:
            term = dot_nn(grad_s[:, start:start + keys.shape[0]], keys)
            grad_q = term if grad_q is None else grad_q + term
            start += keys.shape[0]
        both = jnp.concatenate([grad_s, shares.astype(jnp.bfloat16)], axis=0)
        grad_kv = dot_tn(both, jnp.concatenate([q_only, g_only], axis=0))
        return result, grad_q, grad_kv

    def place(ref, head, index, value, high):
        offset = chunk_offsets(head, stride)[index]
        odd = head % 2 == 1
        if odd != high:
            value = swap(value)
        kept = jnp.where(low, 0.0, value) if odd else jnp.where(low, value, 0.0)
        ref[head // 2, pl.ds(offset, far, stride=stride), :] = kept

    near_grads = []

    def near_head(head):
        keys = kv_near[head]
        q_only, g_only = split(qg_near[head, pl.ds(far, near - far), :])
        result, grad_q, grad_kv = attend(q_only, g_only, [keys], None)
        for index in range(1, stride // R1):
            rows_in = slice((index - 1) * far, index * far)
            place(vf, head, index, result[rows_in], True)
            place(qf, head, index, grad_q[rows_in], False)
        near_grads.append(grad_kv)

    for head in range(early):
        near_head(head)
    pl.semaphore_wait(barrier, len(neighbours))
    for group in range(groups):
        send_own(group)
    handing = [(pass_z, group) for group in range(groups)] + [(pass_x, group) for group in range(groups)]
    late = heads - early
    for head in range(late):
        near_head(early + head)
        while len(handing) * late > 2 * groups * (late - 1 - head):
            step, group = handing.pop(0)
            step(group)
    for step, group in handing:
        step(group)

    total = devices * far
    row_id = lax.broadcasted_iota(jnp.int32, (far, near + total), 0)
    col_id = lax.broadcasted_iota(jnp.int32, (far, near + total), 1)
    ratio = R2 // stride
    twice = (col_id >= near) & (row_id % ratio == 0) & ((col_id - near) % ratio == 0)
    counts = jnp.where(twice, 2.0, 1.0)

    def core_copy(bundle):
        return pltpu.make_async_remote_copy(
            src_ref=part.at[bundle, 1 - outer_id],
            dst_ref=from_core.at[bundle],
            send_sem=send_core.at[bundle],
            recv_sem=recv_core.at[bundle],
            device_id=to_core,
            device_id_type=MESH,
        )

    def x_copy(bundle):
        return pltpu.make_async_remote_copy(
            src_ref=by_x.at[bundle, 1 - my_x],
            dst_ref=from_x.at[bundle],
            send_sem=send_x.at[bundle],
            recv_sem=recv_x.at[bundle],
            device_id=to_x,
            device_id_type=MESH,
        )

    def z_copy(bundle, step, slot):
        return pltpu.make_async_remote_copy(
            src_ref=by_z.at[bundle, peer_z(step)],
            dst_ref=from_z.at[bundle, slot],
            send_sem=send_z.at[bundle, step],
            recv_sem=recv_z.at[bundle, slot],
            device_id=to_z(step),
            device_id_type=MESH,
        )

    def reduce_core(bundle):
        core_copy(bundle).wait_recv()
        both = part[bundle, outer_id].astype(jnp.float32) + from_core[bundle].astype(jnp.float32)
        both = both.astype(jnp.bfloat16).reshape(batch, zs, 2, far, 2 * E)
        for x in range(2):
            by_x[bundle, x] = both[:, :, x]
        x_copy(bundle).start()

    def reduce_x(bundle):
        x_copy(bundle).wait_recv()
        both = by_x[bundle, my_x].astype(jnp.float32) + from_x[bundle].astype(jnp.float32)
        both = both.astype(jnp.bfloat16)
        for inside in range(batch):
            by_z[bundle, :, inside] = both[inside]
        for step in range(1, zs):
            z_copy(bundle, step, my_z).start()

    for head in range(heads):
        if head % group_heads == 0:
            finish_gather(head // group_heads)
        keys = kv_near[head]
        far_keys = kv_far[head // group_heads, :, head % group_heads].reshape(total, 2 * E)
        q_only, g_only = split(qg_near[head, pl.ds(0, far), :])
        result, grad_q, grad_kv = attend(q_only, g_only, [keys, far_keys], counts)
        place(vf, head, 0, result, True)
        place(qf, head, 0, grad_q, False)
        near_grads[head] = near_grads[head] + grad_kv[:near]
        part[head // batch, :, head % batch] = (
            grad_kv[near:].reshape(2, inner, far, 2 * E).astype(jnp.bfloat16)
        )
        if head % batch == batch - 1:
            core_copy(head // batch).start()
            if head // batch >= lag:
                reduce_core(head // batch - lag)

    for bundle in range(max(0, bundles - lag), bundles):
        reduce_core(bundle)
    narrow(out_ref, vf)
    for head in range(heads):
        if head % batch == 0:
            reduce_x(head // batch)
        for index in range(1, stride // R1):
            piece = near_grads[head][index * far:(index + 1) * far]
            place(kf, head, index, piece, False)
            place(gf, head, index, piece, True)
    narrow(gq_ref, qf)
    for head in range(heads):
        bundle, inside = head // batch, head % batch
        piece = near_grads[head][:far] + by_z[bundle, my_z, inside].astype(jnp.float32)
        for step in range(1, zs):
            if inside == 0:
                z_copy(bundle, step, peer_z(step)).wait_recv()
            piece = piece + from_z[bundle, peer_z(step), inside].astype(jnp.float32)
        place(kf, head, 0, piece, False)
        place(gf, head, 0, piece, True)
        if head % 2 == 1:
            narrow_pair(gk_ref, kf, head // 2)
            narrow_pair(gv_ref, gf, head // 2)
    for copy in pending:
        copy.wait_send()
    for bundle in range(bundles):
        core_copy(bundle).wait_send()
        x_copy(bundle).wait_send()
        for step in range(1, zs):
            z_copy(bundle, step, my_z).wait_send()


def store_kernel(*refs):
    sources, targets, sems = refs[:4], refs[4:8], refs[8]
    copies = [
        pltpu.make_async_copy(source, target, sems.at[index])
        for index, (source, target) in enumerate(zip(sources, targets))
    ]
    for copy in copies:
        copy.start()
    for copy in copies:
        copy.wait()


def slide_shards(queries, key_rows, value_rows, grad_out):
    rows, width = queries.shape
    heads = width // E
    inner = lax.axis_size("inner")
    devices = 2 * inner
    zs = inner // 2
    stride = rows * devices // KEYS
    far = rows // stride
    near = rows // R1
    groups = 3
    batch = 2
    bundles = heads // batch
    bf16 = jnp.bfloat16
    whole = pl.BlockSpec(memory_space=pltpu.VMEM)
    dma = pltpu.SemaphoreType.DMA
    results = pl.pallas_call(
        functools.partial(slide_kernel, inner, heads, stride),
        out_shape=[jax.ShapeDtypeStruct((rows, width), bf16)] * 4,
        in_specs=[pl.BlockSpec(memory_space=pltpu.HBM)] * 4,
        out_specs=[whole] * 4,
        scratch_shapes=[pltpu.VMEM((rows, width), bf16)] * 4
        + [dma((4,))]
        + [pltpu.VMEM((heads // 2, rows, 2 * E), jnp.float32)] * 4
        + [pltpu.VMEM((heads, near, 2 * E), bf16)] * 2
        + [
            pltpu.VMEM((groups, devices, heads // groups, far, 2 * E), bf16),
            pltpu.VMEM((bundles, 2, batch, inner, far, 2 * E), bf16),
            pltpu.VMEM((bundles, batch, inner, far, 2 * E), bf16),
            pltpu.VMEM((bundles, 2, batch, zs, far, 2 * E), bf16),
            pltpu.VMEM((bundles, batch, zs, far, 2 * E), bf16),
            pltpu.VMEM((bundles, zs, batch, far, 2 * E), bf16),
            pltpu.VMEM((bundles, zs, batch, far, 2 * E), bf16),
            dma((groups, 4 * zs)),
            dma((groups, devices)),
            dma((bundles,)),
            dma((bundles,)),
            dma((bundles,)),
            dma((bundles,)),
            dma((bundles, zs)),
            dma((bundles, zs)),
        ],
        compiler_params=pltpu.CompilerParams(
            collective_id=0, has_side_effects=True, vmem_limit_bytes=63 * 1024 * 1024
        ),
    )(queries, key_rows, value_rows, grad_out)
    return pl.pallas_call(
        store_kernel,
        out_shape=[jax.ShapeDtypeStruct((rows, width), bf16)] * 4,
        in_specs=[whole] * 4,
        out_specs=[pl.BlockSpec(memory_space=pltpu.HBM)] * 4,
        scratch_shapes=[dma((4,))],
    )(*results)


def shards(queries, key_rows, value_rows, grad_out):
    rows, width = queries.shape
    devices = lax.axis_size("outer") * lax.axis_size("inner")
    stride = rows * devices // KEYS
    one_segment = rows * devices == W2 and rows == W1 and (width // E) % 2 == 0
    nested = stride % R1 == 0 and R2 % stride == 0 and rows % (16 * stride) == 0
    paired = lax.axis_size("outer") == 2 and lax.axis_size("inner") % 2 == 0
    if one_segment and nested and paired and width // E <= stride:
        return slide_shards(queries, key_rows, value_rows, grad_out)
    return general_shards(queries, key_rows, value_rows, grad_out)


def solution(mesh):
    return jax.shard_map(
        shards,
        mesh=mesh,
        in_specs=(
            P(("group", "outer", "inner"), None),
            P(("group", "outer", "inner"), None),
            P(("group", "outer", "inner"), None),
            P(("group", "outer", "inner"), None),
        ),
        out_specs=(
            P(("group", "outer", "inner"), None),
            P(("group", "outer", "inner"), None),
            P(("group", "outer", "inner"), None),
            P(("group", "outer", "inner"), None),
        ),
        check_vma=False,
    )
```
